32 devices in a mesh: gx: 16 (over z, y, x), gy: 2 (over core).
Axes of the slice: x: 2, y: 2, z: 4, core: 2. Of those that a mesh axis runs over, the one named last changes fastest.
Arguments:
- records: float32 [98304, 128], P('gx', 'gy'), may hold values from -1.8 to 1.8
- idents: float32 [65536, 128], P('gx', 'gy'), may hold values from -1.8 to 1.8
- rec_count: int32 [98304], P('gx'), may hold values from 1 to 1000
- id_count: int32 [65536], P('gx'), may hold values from 1 to 1000
- observed: bfloat16 [3072, 128, 128], P('gx'), may hold values from -6 to 6
- send_list: int32 [256, 1], P('gx'), may hold values from 0 to 47
- slot_of_block: int32 [3072], P('gx'), may hold values from 0 to 15, as said below
- id_of_block: int32 [3072], P('gx'), may hold values from 0 to 31
Outputs:
- new_records: float32 [98304, 128], P('gx', 'gy')
- new_idents: float32 [65536, 128], P('gx', 'gy')
The draws below stay inside these ranges and needn't reach their ends.
Inputs may be any that keep to these rules, and one draw needn't show every extreme that they name: `slot_of_block`: each owner's 192 entries use every slot from 0 to 15.
All inputs are finite; a program needn't handle non-finite values.
Results may differ from the reference program's by a relative error of at most 0.013.
Values may be sent and summed in bfloat16 or wider, within the bound.
A program may use at most 128 MiB of HBM per device.

```python
import jax
import jax.numpy as jnp
from jax import lax

RANK = 128
BLK = 128
RB_DEV = 48
IB_DEV = 32
NB_DEV = 192
SLOTS = 1
RECORDS = 98304
IDENTS = 65536
NB_ALL = 3072
PAIRS = 256
N_GX = 16


def draw_slot_of_block(key, part):
    total_slots = N_GX * SLOTS
    row_keys = jax.random.split(jax.random.fold_in(key, 11), N_GX)
    covered = jax.vmap(lambda single: jax.random.permutation(single, total_slots))(row_keys).astype(jnp.int32)
    others = jax.random.randint(jax.random.fold_in(key, 13), (N_GX, NB_DEV - total_slots), 0, total_slots).astype(jnp.int32)
    joined = jnp.concatenate([covered, others], axis=1)
    order_keys = jax.random.split(jax.random.fold_in(key, 17), N_GX)
    orders = jax.vmap(lambda single: jax.random.permutation(single, NB_DEV))(order_keys)
    shuffled = jnp.take_along_axis(joined, orders, axis=1)
    return shuffled.reshape(-1).astype(jnp.int32)


def touch_ends(values, own_key, low, high):
    longest = values.shape.index(max(values.shape))
    spots = []
    for shift in (0, 1):
        where = [jax.random.randint(jax.random.fold_in(own_key, axis), (), 0, length) for axis, length in enumerate(values.shape)]
        where[longest] = (where[longest] + shift) % values.shape[longest]
        spots.append(tuple(where))
    return values.at[spots[0]].set(low).at[spots[1]].set(high)


def block_scale(rng, extent, cuts, low, largest):
    def one(axis_at, shards_of):
        steps = jax.random.uniform(jax.random.fold_in(jax.random.fold_in(rng, 6), axis_at), (shards_of,), jnp.float32, low / len(cuts), largest / len(cuts))
        return jnp.repeat(jnp.exp(steps), extent[axis_at] // shards_of).reshape((-1,) + (1,) * (len(extent) - axis_at - 1))

    loudness = one(*cuts[0])
    for cut in cuts[1:]:
        loudness = loudness * one(*cut)
    return loudness


def noise(own_key, dims, scale, bound, shards=(), kind=jnp.bfloat16):
    drawn = jax.random.normal(own_key, dims, jnp.float32) * scale
    if len(shards) > 0:
        drawn = block_scale(own_key, dims, shards, -0.22, 0.18) * drawn
    return jnp.clip(drawn, min=-bound, max=bound).astype(kind)


def setup_inputs(seed: int = 0) -> dict:
    streams_of = jax.random.split(jax.random.key(seed), 9)
    return {
        "records": noise(streams_of[0], (RECORDS, RANK), 0.3, 1.8, ((0, 16), (1, 2)), jnp.float32),
        "idents": noise(streams_of[1], (IDENTS, RANK), 0.3, 1.8, ((0, 16), (1, 2)), jnp.float32),
        "rec_count": touch_ends(jax.random.randint(streams_of[2], (RECORDS,), 1, 1001), jax.random.fold_in(streams_of[2], 1), 1, 1000).astype(jnp.int32),
        "id_count": touch_ends(jax.random.randint(streams_of[3], (IDENTS,), 1, 1001), jax.random.fold_in(streams_of[3], 1), 1, 1000).astype(jnp.int32),
        "observed": noise(streams_of[4], (NB_ALL, BLK, BLK), 1.0, 6.0, ((0, 16),)),
        "send_list": touch_ends(jax.random.randint(streams_of[5], (PAIRS, SLOTS), 0, RB_DEV), jax.random.fold_in(streams_of[5], 1), 0, RB_DEV - 1).astype(jnp.int32),
        "slot_of_block": draw_slot_of_block(jax.random.fold_in(streams_of[8], 71), 0),
        "id_of_block": touch_ends(jax.random.randint(streams_of[7], (NB_ALL,), 0, IB_DEV), jax.random.fold_in(streams_of[7], 1), 0, IB_DEV - 1).astype(jnp.int32),
    }


def reference(records, idents, rec_count, id_count, observed, send_list, slot_of_block, id_of_block):
    half_cols = RANK // 2
    rec_bf = records.astype(jnp.bfloat16).reshape(N_GX * RB_DEV, BLK, RANK)
    id_bf = idents.astype(jnp.bfloat16).reshape(N_GX * IB_DEV, BLK, RANK)
    rec_weight = (jnp.log1p(rec_count.astype(jnp.float32)) / jnp.log(jnp.float32(1001.0))).astype(jnp.bfloat16)
    rec_weight = rec_weight.astype(jnp.float32).reshape(N_GX * RB_DEV, BLK)
    id_weight = (jnp.log1p(id_count.astype(jnp.float32)) / jnp.log(jnp.float32(1001.0))).reshape(N_GX * IB_DEV, BLK)
    owner = (jnp.arange(N_GX * NB_DEV) // NB_DEV).astype(jnp.int32)
    source = (slot_of_block // SLOTS).astype(jnp.int32)
    position = (slot_of_block % SLOTS).astype(jnp.int32)
    rec_block = (source * RB_DEV + send_list[source * N_GX + owner, position]).astype(jnp.int32)
    id_block = (owner * IB_DEV + id_of_block).astype(jnp.int32)

    def block_step(rec_grad, device):
        start = (device * NB_DEV).astype(jnp.int32)
        my_rec = lax.dynamic_slice_in_dim(rec_block, start, NB_DEV)
        my_id = lax.dynamic_slice_in_dim(id_block, start, NB_DEV)
        my_local = lax.dynamic_slice_in_dim(id_of_block, start, NB_DEV).astype(jnp.int32)
        my_obs = lax.dynamic_slice_in_dim(observed, start, NB_DEV, 0).astype(jnp.float32)
        left_rows = rec_bf[my_rec].astype(jnp.float32)
        right_rows = id_bf[my_id].astype(jnp.float32)
        part_low = jnp.einsum("bik,bjk->bij", left_rows[:, :, :half_cols], right_rows[:, :, :half_cols]).astype(jnp.bfloat16)
        part_high = jnp.einsum("bik,bjk->bij", left_rows[:, :, half_cols:], right_rows[:, :, half_cols:]).astype(jnp.bfloat16)
        weight_grid = rec_weight[my_rec][:, :, None] * id_weight[my_id][:, None, :]
        summed = part_low.astype(jnp.float32) + part_high.astype(jnp.float32)
        resid = (weight_grid * (summed - my_obs)).astype(jnp.bfloat16).astype(jnp.float32)
        grad_left = jnp.einsum("bij,bjk->bik", resid, right_rows)
        grad_right = jnp.einsum("bij,bik->bjk", resid, left_rows)
        rec_grad = rec_grad.at[my_rec].add(grad_left)
        id_part = jnp.zeros((IB_DEV, BLK, RANK), jnp.float32).at[my_local].add(grad_right)
        return rec_grad, id_part

    start_grad = jnp.zeros((N_GX * RB_DEV, BLK, RANK), jnp.float32)
    rec_grad, id_grad = lax.scan(block_step, start_grad, jnp.arange(N_GX, dtype=jnp.int32))
    rec_grad = rec_grad.reshape(records.shape)
    id_grad = id_grad.reshape(idents.shape)
    new_records = records - 0.05 * (rec_grad + 0.1 * records)
    new_idents = idents - 0.05 * (id_grad + 0.1 * idents)
    return new_records, new_idents
```

```python
import jax
import jax.numpy as jnp
from jax import lax
from jax.experimental import pallas as pl
from jax.experimental.pallas import tpu as pltpu
from jax.sharding import PartitionSpec as P

MESH = pl.DeviceIdType.MESH
RATE = 0.05
DECAY = 0.1
UNROLL = 4
F32 = jnp.float32
BF16 = jnp.bfloat16


def dot_nn(a, b):
    return lax.dot_general(a, b, (((1,), (0,)), ((), ())), preferred_element_type=F32)


def dot_nt(a, b):
    return lax.dot_general(a, b, (((1,), (1,)), ((), ())), preferred_element_type=F32)


def log_weight(count):
    return jnp.log(1.0 + count.astype(F32)) / jnp.log(F32(1001.0))


def exchange_kernel(
    send_list, by_slot, by_id, last_slot, last_id, rec_count, id_count,
    rec_hbm, id_hbm, obs_hbm,
    ret_out, new_id_out,
    rec, rec_bf, ids, obs, w_rec, w_id, left, right, w_right, w_left, gram,
    left_send, weight_send, weight_got, back, ret, total, total_gram,
    load_sem, ls, lr, ws, wr, fs, fr, bs, br, rs, rr,
):
    peers = lax.axis_size("gx")
    me = lax.axis_index("gx")
    half = lax.axis_index("gy")
    other = 1 - half
    idents = w_right.shape[0]
    blocks = obs.shape[0]
    blk = obs.shape[1]

    load_rec = pltpu.make_async_copy(rec_hbm, rec, load_sem.at[0])
    load_id = pltpu.make_async_copy(id_hbm, ids, load_sem.at[1])
    load_obs = pltpu.make_async_copy(obs_hbm, obs, load_sem.at[2])
    load_rec.start()
    load_id.start()
    load_obs.start()
    barrier = pltpu.get_barrier_semaphore()

    @pl.loop(1, peers)
    def _(step):
        pl.semaphore_signal(
            barrier, inc=1, device_id={"gx": lax.rem(me + step, peers)}, device_id_type=MESH
        )

    pl.semaphore_signal(barrier, inc=1, device_id={"gy": other}, device_id_type=MESH)

    weights = log_weight(rec_count[...]).astype(BF16).astype(F32)
    for r in range(weights.shape[0]):
        w_rec[r] = weights[r : r + 1, :]
    w_id[...] = log_weight(id_count[...])

    def column(block):
        return pl.ds(pl.multiple_of(block * blk, blk), blk)

    load_rec.wait()

    @pl.loop(0, rec_bf.shape[0])
    def _(r):
        rec_bf[r] = rec[:, column(r)].astype(BF16)

    @pl.loop(0, peers)
    def _(peer):
        wanted = send_list[peer]
        left_send[peer] = rec_bf[wanted]
        weight_send[peer] = w_rec[wanted]

    left[half, me] = left_send[me]
    weight_got[me] = weight_send[me]
    load_id.wait()

    @pl.loop(0, idents)
    def _(c):
        rows = ids[:, column(c)].astype(BF16)
        right[half, c] = rows
        w_right[c] = (rows.astype(F32) * w_id[pl.ds(c, 1), :]).astype(BF16)

    pl.semaphore_wait(barrier, peers)

    def left_copy(peer, slot):
        return pltpu.make_async_remote_copy(
            src_ref=left_send.at[peer], dst_ref=left.at[half, slot],
            send_sem=ls.at[peer], recv_sem=lr.at[slot],
            device_id={"gx": peer}, device_id_type=MESH,
        )

    def weight_copy(peer, slot):
        return pltpu.make_async_remote_copy(
            src_ref=weight_send.at[peer], dst_ref=weight_got.at[slot],
            send_sem=ws.at[peer], recv_sem=wr.at[slot],
            device_id={"gx": peer}, device_id_type=MESH,
        )

    def forward_copy(slot, side):
        return pltpu.make_async_remote_copy(
            src_ref=left.at[side, slot], dst_ref=left.at[side, slot],
            send_sem=fs.at[slot], recv_sem=fr.at[slot],
            device_id={"gy": other}, device_id_type=MESH,
        )

    def back_copy(peer, slot):
        return pltpu.make_async_remote_copy(
            src_ref=back.at[peer], dst_ref=ret.at[slot],
            send_sem=bs.at[peer], recv_sem=br.at[slot],
            device_id={"gx": peer}, device_id_type=MESH,
        )

    def right_copy(side):
        return pltpu.make_async_remote_copy(
            src_ref=right.at[side], dst_ref=right.at[side],
            send_sem=rs, recv_sem=rr,
            device_id={"gy": other}, device_id_type=MESH,
        )

    right_copy(half).start()

    @pl.loop(1, peers)
    def _(step):
        peer = lax.rem(me + step, peers)
        left_copy(peer, me).start()
        weight_copy(peer, me).start()

    forward_copy(me, half).start()

    right_copy(other).wait_recv()

    def full_right(c):
        return jnp.concatenate([right[0, c], right[1, c]], axis=0)

    def full_left(s):
        return jnp.concatenate([left[0, s], left[1, s]], axis=0)

    @pl.loop(0, idents)
    def _(c):
        gram[c] = dot_nt(w_right[c], full_right(c))

    load_obs.wait()

    def running_sums(order, term):
        def step(i, carry):
            acc, acc_gram = carry
            for u in range(UNROLL):
                p = i * UNROLL + u
                code = order[p]
                keep = (code >> 24).astype(F32)
                product, matrix = term((code >> 16) & 255, (code >> 8) & 255, code & 255)
                acc = acc * keep + product
                acc_gram = acc_gram * keep + matrix
                total[p] = acc
                total_gram[p] = acc_gram
            return acc, acc_gram

        zero = jnp.zeros(total.shape[1:], F32)
        lax.fori_loop(0, blocks // UNROLL, step, (zero, zero))

    running_sums(by_slot, lambda b, s, c: (dot_nt(w_right[c], obs[b]), gram[c]))

    def finish_slot(s):
        last = last_slot[s]
        weight = weight_got[s]
        both = full_left(s)
        score = dot_nn(total_gram[last].astype(BF16), both)
        back[s] = ((score - total[last]) * weight).astype(BF16)
        return weight, both

    def left_factors(s, weight, both):
        rows = (left[half, s].astype(F32) * weight).astype(BF16)
        w_left[s] = rows
        gram[s] = dot_nt(rows, both)

    @pl.loop(1, peers)
    def _(step):
        source = lax.rem(me - step + peers, peers)
        left_copy(source, source).wait_recv()
        weight_copy(source, source).wait_recv()
        forward_copy(source, half).start()

    @pl.loop(1, peers)
    def _(step):
        source = lax.rem(me - step + peers, peers)
        forward_copy(source, other).wait_recv()
        finish_slot(source)
        back_copy(source, me).start()

    forward_copy(me, other).wait_recv()
    finish_slot(me)
    ret[me] = back[me]

    @pl.loop(0, peers)
    def _(s):
        left_factors(s, weight_got[s], full_left(s))

    running_sums(by_id, lambda b, s, c: (dot_nn(w_left[s], obs[b]), gram[s]))

    @pl.loop(0, idents)
    def _(c):
        at = last_id[c] >> 1
        used = (last_id[c] & 1).astype(F32)
        score = dot_nn(total_gram[at].astype(BF16), full_right(c))
        grad = (score - total[at]) * (w_id[pl.ds(c, 1), :] * used)
        old = ids[:, column(c)]
        new_id_out[:, column(c)] = old - RATE * (grad + DECAY * old)

    @pl.loop(1, peers)
    def _(step):
        source = lax.rem(me - step + peers, peers)
        back_copy(source, source).wait_recv()

    ret_out[...] = ret[...]

    right_copy(half).wait_send()
    forward_copy(me, half).wait_send()

    @pl.loop(1, peers)
    def _(step):
        peer = lax.rem(me + step, peers)
        left_copy(peer, me).wait_send()
        weight_copy(peer, me).wait_send()
        forward_copy(peer, half).wait_send()
        back_copy(peer, me).wait_send()


def exchange(send_list, by_slot, by_id, last_slot, last_id, rec_count, id_count, rec_t, id_t, obs):
    peers = lax.axis_size("gx")
    half_cols = rec_t.shape[0]
    blocks, blk, _ = obs.shape
    idents = id_count.shape[0]
    smem = pl.BlockSpec(memory_space=pltpu.SMEM)
    vmem = pl.BlockSpec(memory_space=pltpu.VMEM)
    hbm = pl.BlockSpec(memory_space=pl.ANY)
    dma = pltpu.SemaphoreType.DMA
    return pl.pallas_call(
        exchange_kernel,
        out_shape=(
            jax.ShapeDtypeStruct((peers, half_cols, blk), BF16),
            jax.ShapeDtypeStruct(id_t.shape, F32),
        ),
        in_specs=[smem] * 5 + [vmem] * 2 + [hbm] * 3,
        out_specs=(vmem, vmem),
        scratch_shapes=[
            pltpu.VMEM(rec_t.shape, F32),
            pltpu.VMEM((rec_count.shape[0], half_cols, blk), BF16),
            pltpu.VMEM(id_t.shape, F32),
            pltpu.VMEM(obs.shape, BF16),
            pltpu.VMEM((rec_count.shape[0], 1, blk), F32),
            pltpu.VMEM(id_count.shape, F32),
            pltpu.VMEM((2, peers, half_cols, blk), BF16),
            pltpu.VMEM((2, idents, half_cols, blk), BF16),
            pltpu.VMEM((idents, half_cols, blk), BF16),
            pltpu.VMEM((peers, half_cols, blk), BF16),
            pltpu.VMEM((max(idents, peers), half_cols, 2 * half_cols), F32),
            pltpu.VMEM((peers, half_cols, blk), BF16),
            pltpu.VMEM((peers, 1, blk), F32),
            pltpu.VMEM((peers, 1, blk), F32),
            pltpu.VMEM((peers, half_cols, blk), BF16),
            pltpu.VMEM((peers, half_cols, blk), BF16),
            pltpu.VMEM((blocks, half_cols, blk), F32),
            pltpu.VMEM((blocks, half_cols, 2 * half_cols), F32),
            dma((3,)),
        ]
        + [dma((peers,))] * 8
        + [dma, dma],
        compiler_params=pltpu.CompilerParams(
            collective_id=0, has_side_effects=True, vmem_limit_bytes=56 << 20
        ),
        name="exchange",
    )(send_list, by_slot, by_id, last_slot, last_id, rec_count, id_count, rec_t, id_t, obs)


def update_kernel(send_list, rec, ret, new_id, new_rec, id_out, sem):
    blk = ret.shape[2]
    pass_on = pltpu.make_async_copy(new_id, id_out, sem)
    pass_on.start()
    old = rec[...]
    new_rec[...] = old - (RATE * DECAY) * old

    @pl.loop(0, ret.shape[0])
    def _(s):
        cols = pl.ds(pl.multiple_of(send_list[s] * blk, blk), blk)
        new_rec[:, cols] = new_rec[:, cols] - RATE * ret[s].astype(F32)

    pass_on.wait()


def update(send_list, rec_t, ret, new_id):
    vmem = pl.BlockSpec(memory_space=pltpu.VMEM)
    hbm = pl.BlockSpec(memory_space=pl.ANY)
    return pl.pallas_call(
        update_kernel,
        out_shape=(
            jax.ShapeDtypeStruct(rec_t.shape, F32),
            jax.ShapeDtypeStruct(new_id.shape, F32),
        ),
        in_specs=[pl.BlockSpec(memory_space=pltpu.SMEM), vmem, vmem, hbm],
        out_specs=(vmem, hbm),
        scratch_shapes=[pltpu.SemaphoreType.DMA],
        compiler_params=pltpu.CompilerParams(vmem_limit_bytes=32 << 20),
        name="update",
    )(send_list, rec_t, ret, new_id)


def body(records, idents, rec_count, id_count, observed, send_list, slot_of_block, id_of_block):
    peers = lax.axis_size("gx")
    blocks, blk, _ = observed.shape
    id_blocks = idents.shape[0] // blk
    wanted = send_list.reshape(-1)
    place = jnp.arange(blocks, dtype=jnp.int32)
    code = (place << 16) | (slot_of_block << 8) | id_of_block

    def in_order(key):
        same = key[None, :] == key[:, None]
        ahead = place[None, :] < place[:, None]
        earlier = jnp.sum((same & ahead).astype(jnp.int32), axis=1)
        rank = earlier + jnp.sum((key[None, :] < key[:, None]).astype(jnp.int32), axis=1)
        marked = code | (jnp.minimum(earlier, 1) << 24)
        return jnp.sum(jnp.where(rank[:, None] == place[None, :], marked[:, None], 0), axis=0)

    def up_to(key, count):
        below = key[:, None] <= jnp.arange(count, dtype=jnp.int32)[None, :]
        return jnp.sum(below.astype(jnp.int32), axis=0)

    def uses(key, count):
        equal = key[:, None] == jnp.arange(count, dtype=jnp.int32)[None, :]
        return jnp.sum(equal.astype(jnp.int32), axis=0)

    last_slot = up_to(slot_of_block, peers) - 1
    last_id = jnp.maximum(up_to(id_of_block, id_blocks) - 1, 0) * 2
    last_id = last_id + jnp.minimum(uses(id_of_block, id_blocks), 1)
    ret, new_id = exchange(
        wanted,
        in_order(slot_of_block),
        in_order(id_of_block),
        last_slot,
        last_id,
        rec_count.reshape(-1, blk),
        id_count.reshape(-1, blk),
        records.T,
        idents.T,
        observed,
    )
    new_rec, new_id = update(wanted, records.T, ret, new_id)
    return new_rec.T, new_id.T


def solution(mesh):
    in_specs = (
        P("gx", "gy"),
        P("gx", "gy"),
        P("gx"),
        P("gx"),
        P("gx", None, None),
        P("gx", None),
        P("gx"),
        P("gx"),
    )
    out_specs = (P("gx", "gy"), P("gx", "gy"))
    return jax.shard_map(body, mesh=mesh, in_specs=in_specs, out_specs=out_specs, check_vma=False)
```

```python
import jax
import jax.numpy as jnp
from jax import lax
from jax.experimental import pallas as pl
from jax.experimental.pallas import tpu as pltpu
from jax.sharding import PartitionSpec as P

MESH = pl.DeviceIdType.MESH
RATE = 0.05
DECAY = 0.1
UNROLL = 16
GROUP = 4
LANES = 256
F32 = jnp.float32
BF16 = jnp.bfloat16


def dot_nn(a, b):
    return lax.dot_general(a, b, (((1,), (0,)), ((), ())), preferred_element_type=F32)


def dot_nt(a, b):
    return lax.dot_general(a, b, (((1,), (1,)), ((), ())), preferred_element_type=F32)


def log_weight(count):
    return jnp.log(1.0 + count.astype(F32)) / jnp.log(F32(1001.0))


def column_of(row):
    size = row.shape[1]
    diagonal = lax.broadcasted_iota(jnp.int32, (size, size), 0) == lax.broadcasted_iota(
        jnp.int32, (size, size), 1
    )
    return jnp.sum(jnp.where(diagonal, row, 0.0), axis=1, keepdims=True)


def sorted_codes(key, payload):
    size = key.shape[1]
    across = lax.broadcasted_iota(jnp.int32, (size, size), 1)
    ahead = across < lax.broadcasted_iota(jnp.int32, (size, size), 0)
    key_col = column_of(key)
    earlier = jnp.sum(jnp.where((key == key_col) & ahead, 1.0, 0.0), axis=1, keepdims=True)
    rank = earlier + jnp.sum(jnp.where(key < key_col, 1.0, 0.0), axis=1, keepdims=True)
    marked = 2.0 * column_of(payload) + jnp.minimum(earlier, 1.0)
    order = jnp.sum(jnp.where(rank == across.astype(F32), marked, 0.0), axis=0, keepdims=True)
    value = lax.broadcasted_iota(jnp.int32, (1, LANES), 1).astype(F32)
    up_to = jnp.sum(jnp.where(key_col <= value, 1.0, 0.0), axis=0, keepdims=True)
    used = jnp.sum(jnp.where(key_col == value, 1.0, 0.0), axis=0, keepdims=True)
    last = 2.0 * jnp.maximum(up_to - 1.0, 0.0) + jnp.minimum(used, 1.0)
    return order.astype(jnp.int32), last.astype(jnp.int32)


def exchange_kernel(
    send_list, send_row, slot_row, id_row, rec_count, id_count,
    rec_hbm, id_hbm, obs_hbm,
    new_rec_out, new_id_out,
    rec, rec_bf, ids, new_ids, obs, w_rec, w_id, left, right, w_right, w_left, gram,
    left_send, weight_send, weight_got, back, ret, total, total_gram,
    plan, plan_smem, load_sem, ls, lr, ws, wr, fs, fr, bs, br, rs, rr,
):
    peers = lax.axis_size("gx")
    me = lax.axis_index("gx")
    half = lax.axis_index("gy")
    other = 1 - half
    idents = w_right.shape[0]
    blocks = obs.shape[0]
    blk = obs.shape[1]

    load_rec = pltpu.make_async_copy(rec_hbm, rec, load_sem.at[0])
    load_id = pltpu.make_async_copy(id_hbm, ids, load_sem.at[1])
    load_obs = pltpu.make_async_copy(obs_hbm, obs, load_sem.at[2])
    load_rec.start()
    load_id.start()
    load_obs.start()
    barrier = pltpu.get_barrier_semaphore()

    @pl.loop(1, peers)
    def _(step):
        pl.semaphore_signal(
            barrier, inc=1, device_id={"gx": lax.rem(me + step, peers)}, device_id_type=MESH
        )

    pl.semaphore_signal(barrier, inc=1, device_id={"gy": other}, device_id_type=MESH)

    weights = log_weight(rec_count[...]).astype(BF16).astype(F32)
    for r in range(weights.shape[0]):
        w_rec[r] = weights[r : r + 1, :]
    w_id[...] = log_weight(id_count[...])

    place = lax.broadcasted_iota(jnp.int32, (1, blocks), 1)
    code = ((place * 128 + slot_row[...]) * 32 + id_row[...]).astype(F32)
    slots = lax.broadcasted_iota(jnp.int32, (1, peers), 1).astype(F32)
    for row, key, payload in (
        (0, slot_row[...].astype(F32), code),
        (2, id_row[...].astype(F32), code),
        (4, send_row[...].astype(F32), slots),
    ):
        order, last = sorted_codes(key, payload)
        plan[row : row + 1, : order.shape[1]] = order
        plan[row + 1 : row + 2, :] = last
    plan_copy = pltpu.make_async_copy(plan, plan_smem, load_sem.at[3])
    plan_copy.start()

    def within(index, count):
        return jnp.clip(index, 0, count - 1)

    def column(block):
        return pl.ds(pl.multiple_of(block * blk, blk), blk)

    def unrolled(count, function):
        @pl.loop(0, count // GROUP)
        def _(i):
            for u in range(GROUP):
                function(i * GROUP + u)

    load_rec.wait()

    def round_record(r):
        rec_bf[r] = rec[:, column(r)].astype(BF16)

    unrolled(rec_bf.shape[0], round_record)

    @pl.loop(0, peers)
    def _(peer):
        wanted = send_list[peer]
        left_send[peer] = rec_bf[wanted]
        weight_send[peer] = w_rec[wanted]

    left[half, me] = left_send[me]
    weight_got[me] = weight_send[me]
    load_id.wait()

    def round_ident(c):
        rows = ids[:, column(c)].astype(BF16)
        right[half, c] = rows
        w_right[c] = (rows.astype(F32) * w_id[pl.ds(c, 1), :]).astype(BF16)

    unrolled(idents, round_ident)
    pl.semaphore_wait(barrier, peers)

    def left_copy(peer, slot):
        return pltpu.make_async_remote_copy(
            src_ref=left_send.at[peer], dst_ref=left.at[half, slot],
            send_sem=ls.at[peer], recv_sem=lr.at[slot],
            device_id={"gx": peer}, device_id_type=MESH,
        )

    def weight_copy(peer, slot):
        return pltpu.make_async_remote_copy(
            src_ref=weight_send.at[peer], dst_ref=weight_got.at[slot],
            send_sem=ws.at[peer], recv_sem=wr.at[slot],
            device_id={"gx": peer}, device_id_type=MESH,
        )

    def forward_copy(slot, side):
        return pltpu.make_async_remote_copy(
            src_ref=left.at[side, slot], dst_ref=left.at[side, slot],
            send_sem=fs.at[slot], recv_sem=fr.at[slot],
            device_id={"gy": other}, device_id_type=MESH,
        )

    def back_copy(peer, slot):
        return pltpu.make_async_remote_copy(
            src_ref=back.at[peer], dst_ref=ret.at[slot],
            send_sem=bs.at[peer], recv_sem=br.at[slot],
            device_id={"gx": peer}, device_id_type=MESH,
        )

    def right_copy(side):
        return pltpu.make_async_remote_copy(
            src_ref=right.at[side], dst_ref=right.at[side],
            send_sem=rs, recv_sem=rr,
            device_id={"gy": other}, device_id_type=MESH,
        )

    right_copy(half).start()

    @pl.loop(1, peers)
    def _(step):
        peer = lax.rem(me + step, peers)
        left_copy(peer, me).start()
        weight_copy(peer, me).start()

    forward_copy(me, half).start()

    right_copy(other).wait_recv()

    def full_right(c):
        return jnp.concatenate([right[0, c], right[1, c]], axis=0)

    def full_left(s):
        return jnp.concatenate([left[0, s], left[1, s]], axis=0)

    def right_gram(c):
        gram[c] = dot_nt(w_right[c], full_right(c))

    unrolled(idents, right_gram)
    load_obs.wait()
    plan_copy.wait()

    def running_sums(row, term):
        def step(i, carry):
            acc, acc_gram = carry
            for u in range(UNROLL):
                p = i * UNROLL + u
                code = plan_smem[row, p]
                keep = (code & 1).astype(F32)
                product, matrix = term(
                    within(code >> 13, blocks), within((code >> 6) & 127, peers), (code >> 1) & 31
                )
                acc = acc * keep + product
                acc_gram = acc_gram * keep + matrix
                total[p] = acc
                total_gram[p] = acc_gram
            return acc, acc_gram

        zero = jnp.zeros(total.shape[1:], F32)
        lax.fori_loop(0, blocks // UNROLL, step, (zero, zero))

    running_sums(0, lambda b, s, c: (dot_nt(w_right[c], obs[b]), gram[c]))

    def finish_slot(s):
        last = within(plan_smem[1, s] >> 1, blocks)
        score = dot_nn(total_gram[last].astype(BF16), full_left(s))
        back[s] = ((score - total[last]) * weight_got[s]).astype(BF16)

    def left_factors(s):
        rows = (left[half, s].astype(F32) * weight_got[s]).astype(BF16)
        w_left[s] = rows
        gram[s] = dot_nt(rows, full_left(s))

    @pl.loop(1, peers)
    def _(step):
        source = lax.rem(me - step + peers, peers)
        left_copy(source, source).wait_recv()
        weight_copy(source, source).wait_recv()
        forward_copy(source, half).start()

    @pl.loop(0, peers // GROUP)
    def _(i):
        sources = [lax.rem(me - (i * GROUP + u) + peers, peers) for u in range(GROUP)]
        for source in sources:
            forward_copy(source, other).wait_recv()
        for source in sources:
            finish_slot(source)
        for u, source in enumerate(sources):
            if u > 0:
                back_copy(source, me).start()
            else:

                @pl.when(i > 0)
                def _():
                    back_copy(source, me).start()

    ret[me] = back[me]
    unrolled(peers, left_factors)
    running_sums(2, lambda b, s, c: (dot_nn(w_left[s], obs[b]), gram[s]))

    def finish_ident(c):
        at = within(plan_smem[3, c] >> 1, blocks)
        used = (plan_smem[3, c] & 1).astype(F32)
        score = dot_nn(total_gram[at].astype(BF16), full_right(c))
        grad = (score - total[at]) * (w_id[pl.ds(c, 1), :] * used)
        old = ids[:, column(c)]
        new_ids[:, column(c)] = old - RATE * (grad + DECAY * old)

    unrolled(idents, finish_ident)
    store_id = pltpu.make_async_copy(new_ids, new_id_out, load_sem.at[1])
    store_id.start()

    @pl.loop(1, peers)
    def _(step):
        source = lax.rem(me - step + peers, peers)
        back_copy(source, source).wait_recv()

    def add_returned(p, acc):
        code = plan_smem[4, p]
        acc = acc * (code & 1).astype(F32) + ret[within(code >> 1, peers)].astype(F32)
        total[p] = acc
        return acc

    lax.fori_loop(0, peers, add_returned, jnp.zeros(total.shape[1:], F32))

    def finish_record(r):
        at = within(plan_smem[5, r] >> 1, blocks)
        used = (plan_smem[5, r] & 1).astype(F32)
        old = rec[:, column(r)]
        rec[:, column(r)] = old - RATE * (total[at] * used + DECAY * old)

    unrolled(rec_bf.shape[0], finish_record)
    store_rec = pltpu.make_async_copy(rec, new_rec_out, load_sem.at[0])
    store_rec.start()

    right_copy(half).wait_send()
    forward_copy(me, half).wait_send()

    @pl.loop(1, peers)
    def _(step):
        peer = lax.rem(me + step, peers)
        left_copy(peer, me).wait_send()
        weight_copy(peer, me).wait_send()
        forward_copy(peer, half).wait_send()
        back_copy(peer, me).wait_send()

    store_id.wait()
    store_rec.wait()


def exchange(send_list, slot_of_block, id_of_block, rec_count, id_count, rec_t, id_t, obs):
    peers = lax.axis_size("gx")
    half_cols = rec_t.shape[0]
    blocks, blk, _ = obs.shape
    idents = id_count.shape[0]
    smem = pl.BlockSpec(memory_space=pltpu.SMEM)
    vmem = pl.BlockSpec(memory_space=pltpu.VMEM)
    hbm = pl.BlockSpec(memory_space=pl.ANY)
    dma = pltpu.SemaphoreType.DMA
    return pl.pallas_call(
        exchange_kernel,
        out_shape=(
            jax.ShapeDtypeStruct(rec_t.shape, F32),
            jax.ShapeDtypeStruct(id_t.shape, F32),
        ),
        in_specs=[smem] + [vmem] * 5 + [hbm] * 3,
        out_specs=(hbm, hbm),
        scratch_shapes=[
            pltpu.VMEM(rec_t.shape, F32),
            pltpu.VMEM((rec_count.shape[0], half_cols, blk), BF16),
            pltpu.VMEM(id_t.shape, F32),
            pltpu.VMEM(id_t.shape, F32),
            pltpu.VMEM(obs.shape, BF16),
            pltpu.VMEM((rec_count.shape[0], 1, blk), F32),
            pltpu.VMEM(id_count.shape, F32),
            pltpu.VMEM((2, peers, half_cols, blk), BF16),
            pltpu.VMEM((2, idents, half_cols, blk), BF16),
            pltpu.VMEM((idents, half_cols, blk), BF16),
            pltpu.VMEM((peers, half_cols, blk), BF16),
            pltpu.VMEM((max(idents, peers), half_cols, 2 * half_cols), F32),
            pltpu.VMEM((peers, half_cols, blk), BF16),
            pltpu.VMEM((peers, 1, blk), F32),
            pltpu.VMEM((peers, 1, blk), F32),
            pltpu.VMEM((peers, half_cols, blk), BF16),
            pltpu.VMEM((peers, half_cols, blk), BF16),
            pltpu.VMEM((blocks, half_cols, blk), F32),
            pltpu.VMEM((blocks, half_cols, 2 * half_cols), F32),
            pltpu.VMEM((8, LANES), jnp.int32),
            pltpu.SMEM((8, LANES), jnp.int32),
            dma((4,)),
        ]
        + [dma((peers,))] * 8
        + [dma, dma],
        compiler_params=pltpu.CompilerParams(
            collective_id=0, has_side_effects=True, vmem_limit_bytes=56 << 20
        ),
        name="exchange",
    )(
        send_list, send_list[None], slot_of_block[None], id_of_block[None],
        rec_count, id_count, rec_t, id_t, obs,
    )


def body(records, idents, rec_count, id_count, observed, send_list, slot_of_block, id_of_block):
    blk = observed.shape[1]
    new_rec, new_id = exchange(
        send_list.reshape(-1),
        slot_of_block,
        id_of_block,
        rec_count.reshape(-1, blk),
        id_count.reshape(-1, blk),
        records.T,
        idents.T,
        observed,
    )
    return new_rec.T, new_id.T


def solution(mesh):
    in_specs = (
        P("gx", "gy"),
        P("gx", "gy"),
        P("gx"),
        P("gx"),
        P("gx", None, None),
        P("gx", None),
        P("gx"),
        P("gx"),
    )
    out_specs = (P("gx", "gy"), P("gx", "gy"))
    return jax.shard_map(body, mesh=mesh, in_specs=in_specs, out_specs=out_specs, check_vma=False)
```

```python
import jax
import jax.numpy as jnp
from jax import lax
from jax.experimental import pallas as pl
from jax.experimental.pallas import tpu as pltpu
from jax.sharding import PartitionSpec as P

MESH = pl.DeviceIdType.MESH
RATE = 0.05
DECAY = 0.1
UNROLL = 16
GROUP = 4
PARTS = 4
LANES = 256
F32 = jnp.float32
BF16 = jnp.bfloat16


def dot_nn(a, b):
    return lax.dot_general(a, b, (((1,), (0,)), ((), ())), preferred_element_type=F32)


def dot_nt(a, b):
    return lax.dot_general(a, b, (((1,), (1,)), ((), ())), preferred_element_type=F32)


def log_weight(count):
    return jnp.log(1.0 + count.astype(F32)) / jnp.log(F32(1001.0))


def column_of(row):
    size = row.shape[1]
    diagonal = lax.broadcasted_iota(jnp.int32, (size, size), 0) == lax.broadcasted_iota(
        jnp.int32, (size, size), 1
    )
    return jnp.sum(jnp.where(diagonal, row, 0.0), axis=1, keepdims=True)


def sorted_codes(key, payload):
    size = key.shape[1]
    across = lax.broadcasted_iota(jnp.int32, (size, size), 1)
    ahead = across < lax.broadcasted_iota(jnp.int32, (size, size), 0)
    key_col = column_of(key)
    earlier = jnp.sum(jnp.where((key == key_col) & ahead, 1.0, 0.0), axis=1, keepdims=True)
    rank = earlier + jnp.sum(jnp.where(key < key_col, 1.0, 0.0), axis=1, keepdims=True)
    marked = 2.0 * column_of(payload) + jnp.minimum(earlier, 1.0)
    order = jnp.sum(jnp.where(rank == across.astype(F32), marked, 0.0), axis=0, keepdims=True)
    value = lax.broadcasted_iota(jnp.int32, (1, LANES), 1).astype(F32)
    up_to = jnp.sum(jnp.where(key_col <= value, 1.0, 0.0), axis=0, keepdims=True)
    used = jnp.sum(jnp.where(key_col == value, 1.0, 0.0), axis=0, keepdims=True)
    last = 2.0 * jnp.maximum(up_to - 1.0, 0.0) + jnp.minimum(used, 1.0)
    return order.astype(jnp.int32), last.astype(jnp.int32)


def exchange_kernel(
    send_list, slot_row, id_row, rec_count, id_count,
    rec_hbm, id_hbm, obs_hbm,
    ret_out, new_id_out,
    rec, rec_bf, ids, new_ids, obs, w_rec, w_id, left, right, w_right, w_left, gram,
    left_send, weight_send, weight_got, back, ret, total, total_gram,
    plan, plan_smem, load_sem, ls, lr, ws, wr, fs, fr, bs, br, rs, rr,
):
    peers = lax.axis_size("gx")
    me = lax.axis_index("gx")
    half = lax.axis_index("gy")
    other = 1 - half
    idents = w_right.shape[0]
    blocks = obs.shape[0]
    blk = obs.shape[1]

    load_rec = pltpu.make_async_copy(rec_hbm, rec, load_sem.at[0])
    load_id = pltpu.make_async_copy(id_hbm, ids, load_sem.at[1])
    load_obs = pltpu.make_async_copy(obs_hbm, obs, load_sem.at[2])
    load_rec.start()
    load_id.start()
    barrier = pltpu.get_barrier_semaphore()

    @pl.loop(1, peers)
    def _(step):
        pl.semaphore_signal(
            barrier, inc=1, device_id={"gx": lax.rem(me + step, peers)}, device_id_type=MESH
        )

    pl.semaphore_signal(barrier, inc=1, device_id={"gy": other}, device_id_type=MESH)

    weights = log_weight(rec_count[...]).astype(BF16).astype(F32)
    for r in range(weights.shape[0]):
        w_rec[r] = weights[r : r + 1, :]

    def within(index, count):
        return jnp.clip(index, 0, count - 1)

    def column(block):
        return pl.ds(pl.multiple_of(block * blk, blk), blk)

    def unrolled(count, function):
        @pl.loop(0, count // GROUP)
        def _(i):
            for u in range(GROUP):
                function(i * GROUP + u)

    load_rec.wait()
    load_obs.start()

    def round_record(r):
        rec_bf[r] = rec[:, column(r)].astype(BF16)

    unrolled(rec_bf.shape[0], round_record)

    @pl.loop(0, peers)
    def _(peer):
        wanted = send_list[peer]
        left_send[peer] = rec_bf[wanted]
        weight_send[peer] = w_rec[wanted]

    left[half, me] = left_send[me]
    weight_got[me] = weight_send[me]
    pl.semaphore_wait(barrier, peers)

    def left_copy(peer, slot):
        return pltpu.make_async_remote_copy(
            src_ref=left_send.at[peer], dst_ref=left.at[half, slot],
            send_sem=ls.at[peer], recv_sem=lr.at[slot],
            device_id={"gx": peer}, device_id_type=MESH,
        )

    def weight_copy(peer, slot):
        return pltpu.make_async_remote_copy(
            src_ref=weight_send.at[peer], dst_ref=weight_got.at[slot],
            send_sem=ws.at[peer], recv_sem=wr.at[slot],
            device_id={"gx": peer}, device_id_type=MESH,
        )

    def forward_copy(slot, side):
        return pltpu.make_async_remote_copy(
            src_ref=left.at[side, slot], dst_ref=left.at[side, slot],
            send_sem=fs.at[slot], recv_sem=fr.at[slot],
            device_id={"gy": other}, device_id_type=MESH,
        )

    def back_copy(peer, slot):
        return pltpu.make_async_remote_copy(
            src_ref=back.at[peer], dst_ref=ret.at[slot],
            send_sem=bs.at[peer], recv_sem=br.at[slot],
            device_id={"gx": peer}, device_id_type=MESH,
        )

    def right_copy(side):
        return pltpu.make_async_remote_copy(
            src_ref=right.at[side], dst_ref=right.at[side],
            send_sem=rs, recv_sem=rr,
            device_id={"gy": other}, device_id_type=MESH,
        )

    @pl.loop(1, peers)
    def _(step):
        peer = lax.rem(me + step, peers)
        left_copy(peer, me).start()
        weight_copy(peer, me).start()

    forward_copy(me, half).start()
    load_id.wait()
    w_id[...] = log_weight(id_count[...])

    def round_ident(c):
        rows = ids[:, column(c)].astype(BF16)
        right[half, c] = rows
        w_right[c] = (rows.astype(F32) * w_id[pl.ds(c, 1), :]).astype(BF16)

    unrolled(idents, round_ident)
    right_copy(half).start()

    place = lax.broadcasted_iota(jnp.int32, (1, blocks), 1)
    code = ((place * 128 + slot_row[...]) * 32 + id_row[...]).astype(F32)
    for row, key, payload in (
        (0, slot_row[...].astype(F32), code),
        (2, id_row[...].astype(F32), code),
    ):
        order, last = sorted_codes(key, payload)
        plan[row : row + 1, : order.shape[1]] = order
        plan[row + 1 : row + 2, :] = last
    plan_copy = pltpu.make_async_copy(plan, plan_smem, load_sem.at[3])
    plan_copy.start()


    right_copy(other).wait_recv()

    def full_right(c):
        return jnp.concatenate([right[0, c], right[1, c]], axis=0)

    def full_left(s):
        return jnp.concatenate([left[0, s], left[1, s]], axis=0)

    def right_gram(c):
        gram[c] = dot_nt(w_right[c], full_right(c))

    unrolled(idents, right_gram)
    load_obs.wait()
    plan_copy.wait()

    def running_sums(row, term):
        def step(i, carry):
            acc, acc_gram = carry
            for u in range(UNROLL):
                p = i * UNROLL + u
                code = plan_smem[row, p]
                keep = (code & 1).astype(F32)
                product, matrix = term(
                    within(code >> 13, blocks), within((code >> 6) & 127, peers), (code >> 1) & 31
                )
                acc = acc * keep + product
                acc_gram = acc_gram * keep + matrix
                total[p] = acc
                total_gram[p] = acc_gram
            return acc, acc_gram

        zero = jnp.zeros(total.shape[1:], F32)
        lax.fori_loop(0, blocks // UNROLL, step, (zero, zero))

    running_sums(0, lambda b, s, c: (dot_nt(w_right[c], obs[b]), gram[c]))

    def finish_slot(s):
        last = within(plan_smem[1, s] >> 1, blocks)
        score = dot_nn(total_gram[last].astype(BF16), full_left(s))
        back[s] = ((score - total[last]) * weight_got[s]).astype(BF16)

    def left_factors(s):
        rows = (left[half, s].astype(F32) * weight_got[s]).astype(BF16)
        w_left[s] = rows
        gram[s] = dot_nt(rows, full_left(s))

    @pl.loop(1, peers)
    def _(step):
        source = lax.rem(me - step + peers, peers)
        left_copy(source, source).wait_recv()
        weight_copy(source, source).wait_recv()
        forward_copy(source, half).start()

    @pl.loop(0, peers // GROUP)
    def _(i):
        sources = [lax.rem(me - (i * GROUP + u) + peers, peers) for u in range(GROUP)]
        for source in sources:
            forward_copy(source, other).wait_recv()
        for source in sources:
            finish_slot(source)
        for u, source in enumerate(sources):
            if u > 0:
                back_copy(source, me).start()
            else:

                @pl.when(i > 0)
                def _():
                    back_copy(source, me).start()

    ret[me] = back[me]
    unrolled(peers, left_factors)
    running_sums(2, lambda b, s, c: (dot_nn(w_left[s], obs[b]), gram[s]))

    def finish_ident(c):
        at = within(plan_smem[3, c] >> 1, blocks)
        used = (plan_smem[3, c] & 1).astype(F32)
        score = dot_nn(total_gram[at].astype(BF16), full_right(c))
        grad = (score - total[at]) * (w_id[pl.ds(c, 1), :] * used)
        old = ids[:, column(c)]
        new_ids[:, column(c)] = old - RATE * (grad + DECAY * old)

    unrolled(idents, finish_ident)
    store_id = pltpu.make_async_copy(new_ids, new_id_out, load_sem.at[1])
    store_id.start()

    @pl.loop(1, peers)
    def _(step):
        source = lax.rem(me - step + peers, peers)
        back_copy(source, source).wait_recv()

    store_ret = pltpu.make_async_copy(ret, ret_out, load_sem.at[0])
    store_ret.start()

    right_copy(half).wait_send()
    forward_copy(me, half).wait_send()

    @pl.loop(1, peers)
    def _(step):
        peer = lax.rem(me + step, peers)
        left_copy(peer, me).wait_send()
        weight_copy(peer, me).wait_send()
        forward_copy(peer, half).wait_send()
        back_copy(peer, me).wait_send()

    store_id.wait()
    store_ret.wait()


def exchange(send_list, slot_of_block, id_of_block, rec_count, id_count, rec_t, id_t, obs):
    peers = lax.axis_size("gx")
    half_cols = rec_t.shape[0]
    blocks, blk, _ = obs.shape
    idents = id_count.shape[0]
    smem = pl.BlockSpec(memory_space=pltpu.SMEM)
    vmem = pl.BlockSpec(memory_space=pltpu.VMEM)
    hbm = pl.BlockSpec(memory_space=pltpu.HBM)
    anywhere = pl.BlockSpec(memory_space=pl.ANY)
    dma = pltpu.SemaphoreType.DMA
    return pl.pallas_call(
        exchange_kernel,
        out_shape=(
            jax.ShapeDtypeStruct((peers, half_cols, blk), BF16),
            jax.ShapeDtypeStruct(id_t.shape, F32),
        ),
        in_specs=[smem] + [vmem] * 4 + [hbm] * 3,
        out_specs=(anywhere, anywhere),
        scratch_shapes=[
            pltpu.VMEM(rec_t.shape, F32),
            pltpu.VMEM((rec_count.shape[0], half_cols, blk), BF16),
            pltpu.VMEM(id_t.shape, F32),
            pltpu.VMEM(id_t.shape, F32),
            pltpu.VMEM(obs.shape, BF16),
            pltpu.VMEM((rec_count.shape[0], 1, blk), F32),
            pltpu.VMEM(id_count.shape, F32),
            pltpu.VMEM((2, peers, half_cols, blk), BF16),
            pltpu.VMEM((2, idents, half_cols, blk), BF16),
            pltpu.VMEM((idents, half_cols, blk), BF16),
            pltpu.VMEM((peers, half_cols, blk), BF16),
            pltpu.VMEM((max(idents, peers), half_cols, 2 * half_cols), F32),
            pltpu.VMEM((peers, half_cols, blk), BF16),
            pltpu.VMEM((peers, 1, blk), F32),
            pltpu.VMEM((peers, 1, blk), F32),
            pltpu.VMEM((peers, half_cols, blk), BF16),
            pltpu.VMEM((peers, half_cols, blk), BF16),
            pltpu.VMEM((blocks, half_cols, blk), F32),
            pltpu.VMEM((blocks, half_cols, 2 * half_cols), F32),
            pltpu.VMEM((8, LANES), jnp.int32),
            pltpu.SMEM((8, LANES), jnp.int32),
            dma((4,)),
        ]
        + [dma((peers,))] * 8
        + [dma, dma],
        compiler_params=pltpu.CompilerParams(
            collective_id=0, has_side_effects=True, vmem_limit_bytes=(32 << 20) + (peers << 17)
        ),
        name="exchange",
    )(
        send_list, slot_of_block[None], id_of_block[None],
        rec_count, id_count, rec_t, id_t, obs,
    )


def update_kernel(send_list, rec_in, ret_in, new_id, new_rec, id_out, rec, ret, sem, parts):
    blk = ret.shape[2]
    width = rec.shape[1] // PARTS

    def part(k):
        return pl.ds(k * width, width)

    def load(k):
        return pltpu.make_async_copy(rec_in.at[:, part(k)], rec.at[:, part(k)], parts.at[k])

    def store(k):
        return pltpu.make_async_copy(rec.at[:, part(k)], new_rec.at[:, part(k)], parts.at[k])

    load_ret = pltpu.make_async_copy(ret_in, ret, sem.at[0])
    pass_on = pltpu.make_async_copy(new_id, id_out, sem.at[1])
    for k in range(PARTS):
        load(k).start()
    load_ret.start()
    pass_on.start()
    for k in range(PARTS):
        load(k).wait()
    load_ret.wait()
    shrink = 1.0 - RATE * DECAY

    @pl.loop(0, ret.shape[0])
    def _(s):
        cols = pl.ds(pl.multiple_of(send_list[s] * blk, blk), blk)
        rec[:, cols] = rec[:, cols] - (RATE / shrink) * ret[s].astype(F32)

    for k in range(PARTS):
        rec[:, part(k)] = rec[:, part(k)] * shrink
        store(k).start()
    for k in range(PARTS):
        store(k).wait()
    pass_on.wait()


def update(send_list, rec_t, ret, new_id):
    hbm = pl.BlockSpec(memory_space=pltpu.HBM)
    anywhere = pl.BlockSpec(memory_space=pl.ANY)
    dma = pltpu.SemaphoreType.DMA
    return pl.pallas_call(
        update_kernel,
        out_shape=(
            jax.ShapeDtypeStruct(rec_t.shape, F32),
            jax.ShapeDtypeStruct(new_id.shape, F32),
        ),
        in_specs=[pl.BlockSpec(memory_space=pltpu.SMEM)] + [anywhere] * 3,
        out_specs=(hbm, hbm),
        scratch_shapes=[
            pltpu.VMEM(rec_t.shape, F32),
            pltpu.VMEM(ret.shape, BF16),
            dma((2,)),
            dma((PARTS,)),
        ],
        compiler_params=pltpu.CompilerParams(vmem_limit_bytes=16 << 20),
        name="update",
    )(send_list, rec_t, ret, new_id)


def body(records, idents, rec_count, id_count, observed, send_list, slot_of_block, id_of_block):
    blk = observed.shape[1]
    wanted = send_list.reshape(-1)
    rec_t = records.T
    ret, new_id = exchange(
        wanted,
        slot_of_block,
        id_of_block,
        rec_count.reshape(-1, blk),
        id_count.reshape(-1, blk),
        rec_t,
        idents.T,
        observed,
    )
    new_rec, new_id = update(wanted, rec_t, ret, new_id)
    return new_rec.T, new_id.T


def solution(mesh):
    in_specs = (
        P("gx", "gy"),
        P("gx", "gy"),
        P("gx"),
        P("gx"),
        P("gx", None, None),
        P("gx", None),
        P("gx"),
        P("gx"),
    )
    out_specs = (P("gx", "gy"), P("gx", "gy"))
    return jax.shard_map(body, mesh=mesh, in_specs=in_specs, out_specs=out_specs, check_vma=False)
```

```python
import jax
import jax.numpy as jnp
from jax import lax
from jax.experimental import pallas as pl
from jax.experimental.pallas import tpu as pltpu
from jax.sharding import PartitionSpec as P

MESH = pl.DeviceIdType.MESH
RATE = 0.05
DECAY = 0.1
UNROLL = 16
GROUP = 4
PARTS = 4
VMEM_BYTES = 58 << 20
LANES = 256
F32 = jnp.float32
BF16 = jnp.bfloat16


def dot_nn(a, b):
    return lax.dot_general(a, b, (((1,), (0,)), ((), ())), preferred_element_type=F32)


def dot_nt(a, b):
    return lax.dot_general(a, b, (((1,), (1,)), ((), ())), preferred_element_type=F32)


def log_weight(count):
    return jnp.log(1.0 + count.astype(F32)) / jnp.log(F32(1001.0))


def column_of(row):
    size = row.shape[1]
    diagonal = lax.broadcasted_iota(jnp.int32, (size, size), 0) == lax.broadcasted_iota(
        jnp.int32, (size, size), 1
    )
    return jnp.sum(jnp.where(diagonal, row, 0.0), axis=1, keepdims=True)


def sorted_codes(key, payload):
    size = key.shape[1]
    across = lax.broadcasted_iota(jnp.int32, (size, size), 1)
    ahead = across < lax.broadcasted_iota(jnp.int32, (size, size), 0)
    key_col = column_of(key)
    earlier = jnp.sum(jnp.where((key == key_col) & ahead, 1.0, 0.0), axis=1, keepdims=True)
    rank = earlier + jnp.sum(jnp.where(key < key_col, 1.0, 0.0), axis=1, keepdims=True)
    marked = 2.0 * column_of(payload) + jnp.minimum(earlier, 1.0)
    order = jnp.sum(jnp.where(rank == across.astype(F32), marked, 0.0), axis=0, keepdims=True)
    value = lax.broadcasted_iota(jnp.int32, (1, LANES), 1).astype(F32)
    up_to = jnp.sum(jnp.where(key_col <= value, 1.0, 0.0), axis=0, keepdims=True)
    used = jnp.sum(jnp.where(key_col == value, 1.0, 0.0), axis=0, keepdims=True)
    last = 2.0 * jnp.maximum(up_to - 1.0, 0.0) + jnp.minimum(used, 1.0)
    return order.astype(jnp.int32), last.astype(jnp.int32)


def exchange_kernel(
    send_list, slot_row, id_row, rec_count, id_count,
    rec_hbm, id_hbm, obs_hbm,
    ret_out, new_id_out,
    rec, rec_bf, ids, new_ids, obs, w_rec, w_id, left, right, w_right, w_left, gram,
    left_send, weight_send, weight_got, back, ret, total, total_gram,
    plan, plan_smem, load_sem, ls, lr, ws, wr, fs, fr, bs, br, rs, rr,
):
    peers = lax.axis_size("gx")
    me = lax.axis_index("gx")
    half = lax.axis_index("gy")
    other = 1 - half
    idents = w_right.shape[0]
    blocks = obs.shape[0]
    blk = obs.shape[1]

    load_rec = pltpu.make_async_copy(rec_hbm, rec, load_sem.at[0])
    load_id = pltpu.make_async_copy(id_hbm, ids, load_sem.at[1])
    load_obs = pltpu.make_async_copy(obs_hbm, obs, load_sem.at[2])
    load_rec.start()
    load_id.start()
    barrier = pltpu.get_barrier_semaphore()

    @pl.loop(1, peers)
    def _(step):
        pl.semaphore_signal(
            barrier, inc=1, device_id={"gx": lax.rem(me + step, peers)}, device_id_type=MESH
        )

    pl.semaphore_signal(barrier, inc=1, device_id={"gy": other}, device_id_type=MESH)

    weights = log_weight(rec_count[...]).astype(BF16).astype(F32)
    for r in range(weights.shape[0]):
        w_rec[r] = weights[r : r + 1, :]

    def within(index, count):
        return jnp.clip(index, 0, count - 1)

    def column(block):
        return pl.ds(pl.multiple_of(block * blk, blk), blk)

    def unrolled(count, function):
        @pl.loop(0, count // GROUP)
        def _(i):
            for u in range(GROUP):
                function(i * GROUP + u)

    load_rec.wait()
    load_obs.start()

    def round_record(r):
        rec_bf[r] = rec[:, column(r)].astype(BF16)

    unrolled(rec_bf.shape[0], round_record)

    @pl.loop(0, peers)
    def _(peer):
        wanted = send_list[peer]
        left_send[peer] = rec_bf[wanted]
        weight_send[peer] = w_rec[wanted]

    left[half, me] = left_send[me]
    weight_got[me] = weight_send[me]
    pl.semaphore_wait(barrier, peers)

    def left_copy(peer, slot):
        return pltpu.make_async_remote_copy(
            src_ref=left_send.at[peer], dst_ref=left.at[half, slot],
            send_sem=ls.at[peer], recv_sem=lr.at[slot],
            device_id={"gx": peer}, device_id_type=MESH,
        )

    def weight_copy(peer, slot):
        return pltpu.make_async_remote_copy(
            src_ref=weight_send.at[peer], dst_ref=weight_got.at[slot],
            send_sem=ws.at[peer], recv_sem=wr.at[slot],
            device_id={"gx": peer}, device_id_type=MESH,
        )

    def forward_copy(slot, side):
        return pltpu.make_async_remote_copy(
            src_ref=left.at[side, slot], dst_ref=left.at[side, slot],
            send_sem=fs.at[slot], recv_sem=fr.at[slot],
            device_id={"gy": other}, device_id_type=MESH,
        )

    def back_copy(peer, slot):
        return pltpu.make_async_remote_copy(
            src_ref=back.at[peer], dst_ref=ret.at[slot],
            send_sem=bs.at[peer], recv_sem=br.at[slot],
            device_id={"gx": peer}, device_id_type=MESH,
        )

    def right_copy(side):
        return pltpu.make_async_remote_copy(
            src_ref=right.at[side], dst_ref=right.at[side],
            send_sem=rs, recv_sem=rr,
            device_id={"gy": other}, device_id_type=MESH,
        )

    @pl.loop(1, peers)
    def _(step):
        peer = lax.rem(me + step, peers)
        left_copy(peer, me).start()
        weight_copy(peer, me).start()

    forward_copy(me, half).start()
    load_id.wait()
    w_id[...] = log_weight(id_count[...])

    def round_ident(c):
        rows = ids[:, column(c)].astype(BF16)
        right[half, c] = rows
        w_right[c] = (rows.astype(F32) * w_id[pl.ds(c, 1), :]).astype(BF16)

    unrolled(idents, round_ident)
    right_copy(half).start()

    place = lax.broadcasted_iota(jnp.int32, (1, blocks), 1)
    code = ((place * 128 + slot_row[...]) * 32 + id_row[...]).astype(F32)
    for row, key, payload in (
        (0, slot_row[...].astype(F32), code),
        (2, id_row[...].astype(F32), code),
    ):
        order, last = sorted_codes(key, payload)
        plan[row : row + 1, : order.shape[1]] = order
        plan[row + 1 : row + 2, :] = last
    plan_copy = pltpu.make_async_copy(plan, plan_smem, load_sem.at[3])
    plan_copy.start()


    right_copy(other).wait_recv()

    def full_right(c):
        return jnp.concatenate([right[0, c], right[1, c]], axis=0)

    def full_left(s):
        return jnp.concatenate([left[0, s], left[1, s]], axis=0)

    def right_gram(c):
        gram[c] = dot_nt(w_right[c], full_right(c))

    unrolled(idents, right_gram)
    load_obs.wait()
    plan_copy.wait()

    def running_sums(row, term):
        def step(i, carry):
            acc, acc_gram = carry
            for u in range(UNROLL):
                p = i * UNROLL + u
                code = plan_smem[row, p]
                keep = (code & 1).astype(F32)
                product, matrix = term(
                    within(code >> 13, blocks), within((code >> 6) & 127, peers), (code >> 1) & 31
                )
                acc = acc * keep + product
                acc_gram = acc_gram * keep + matrix
                total[p] = acc
                total_gram[p] = acc_gram
            return acc, acc_gram

        zero = jnp.zeros(total.shape[1:], F32)
        lax.fori_loop(0, blocks // UNROLL, step, (zero, zero))

    running_sums(0, lambda b, s, c: (dot_nt(w_right[c], obs[b]), gram[c]))

    def finish_slot(s):
        last = within(plan_smem[1, s] >> 1, blocks)
        score = dot_nn(total_gram[last].astype(BF16), full_left(s))
        back[s] = ((score - total[last]) * weight_got[s]).astype(BF16)

    def left_factors(s):
        rows = (left[half, s].astype(F32) * weight_got[s]).astype(BF16)
        w_left[s] = rows
        gram[s] = dot_nt(rows, full_left(s))

    @pl.loop(1, peers)
    def _(step):
        source = lax.rem(me - step + peers, peers)
        left_copy(source, source).wait_recv()
        weight_copy(source, source).wait_recv()
        forward_copy(source, half).start()

    @pl.loop(0, peers // GROUP)
    def _(i):
        sources = [lax.rem(me - (i * GROUP + u) + peers, peers) for u in range(GROUP)]
        for source in sources:
            forward_copy(source, other).wait_recv()
        for source in sources:
            finish_slot(source)
        for u, source in enumerate(sources):
            if u > 0:
                back_copy(source, me).start()
            else:

                @pl.when(i > 0)
                def _():
                    back_copy(source, me).start()

    ret[me] = back[me]
    unrolled(peers, left_factors)
    running_sums(2, lambda b, s, c: (dot_nn(w_left[s], obs[b]), gram[s]))

    def finish_ident(c):
        at = within(plan_smem[3, c] >> 1, blocks)
        used = (plan_smem[3, c] & 1).astype(F32)
        score = dot_nn(total_gram[at].astype(BF16), full_right(c))
        grad = (score - total[at]) * (w_id[pl.ds(c, 1), :] * used)
        old = ids[:, column(c)]
        new_ids[:, column(c)] = old - RATE * (grad + DECAY * old)

    unrolled(idents, finish_ident)
    store_id = pltpu.make_async_copy(new_ids, new_id_out, load_sem.at[1])
    store_id.start()

    @pl.loop(1, peers)
    def _(step):
        source = lax.rem(me - step + peers, peers)
        back_copy(source, source).wait_recv()

    store_ret = pltpu.make_async_copy(ret, ret_out, load_sem.at[0])
    store_ret.start()

    right_copy(half).wait_send()
    forward_copy(me, half).wait_send()

    @pl.loop(1, peers)
    def _(step):
        peer = lax.rem(me + step, peers)
        left_copy(peer, me).wait_send()
        weight_copy(peer, me).wait_send()
        forward_copy(peer, half).wait_send()
        back_copy(peer, me).wait_send()

    store_id.wait()
    store_ret.wait()


def exchange(send_list, slot_of_block, id_of_block, rec_count, id_count, rec_t, id_t, obs):
    peers = lax.axis_size("gx")
    half_cols = rec_t.shape[0]
    blocks, blk, _ = obs.shape
    idents = id_count.shape[0]
    smem = pl.BlockSpec(memory_space=pltpu.SMEM)
    vmem = pl.BlockSpec(memory_space=pltpu.VMEM)
    hbm = pl.BlockSpec(memory_space=pltpu.HBM)
    anywhere = pl.BlockSpec(memory_space=pl.ANY)
    dma = pltpu.SemaphoreType.DMA
    return pl.pallas_call(
        exchange_kernel,
        out_shape=(
            jax.ShapeDtypeStruct((peers, half_cols, blk), BF16),
            jax.ShapeDtypeStruct(id_t.shape, F32),
        ),
        in_specs=[smem] + [vmem] * 4 + [hbm] * 3,
        out_specs=(anywhere, anywhere),
        scratch_shapes=[
            pltpu.VMEM(rec_t.shape, F32),
            pltpu.VMEM((rec_count.shape[0], half_cols, blk), BF16),
            pltpu.VMEM(id_t.shape, F32),
            pltpu.VMEM(id_t.shape, F32),
            pltpu.VMEM(obs.shape, BF16),
            pltpu.VMEM((rec_count.shape[0], 1, blk), F32),
            pltpu.VMEM(id_count.shape, F32),
            pltpu.VMEM((2, peers, half_cols, blk), BF16),
            pltpu.VMEM((2, idents, half_cols, blk), BF16),
            pltpu.VMEM((idents, half_cols, blk), BF16),
            pltpu.VMEM((peers, half_cols, blk), BF16),
            pltpu.VMEM((max(idents, peers), half_cols, 2 * half_cols), F32),
            pltpu.VMEM((peers, half_cols, blk), BF16),
            pltpu.VMEM((peers, 1, blk), F32),
            pltpu.VMEM((peers, 1, blk), F32),
            pltpu.VMEM((peers, half_cols, blk), BF16),
            pltpu.VMEM((peers, half_cols, blk), BF16),
            pltpu.VMEM((blocks, half_cols, blk), F32),
            pltpu.VMEM((blocks, half_cols, 2 * half_cols), F32),
            pltpu.VMEM((8, LANES), jnp.int32),
            pltpu.SMEM((8, LANES), jnp.int32),
            dma((4,)),
        ]
        + [dma((peers,))] * 8
        + [dma, dma],
        compiler_params=pltpu.CompilerParams(
            collective_id=0, has_side_effects=True, vmem_limit_bytes=VMEM_BYTES
        ),
        name="exchange",
    )(
        send_list, slot_of_block[None], id_of_block[None],
        rec_count, id_count, rec_t, id_t, obs,
    )


def update_kernel(send_list, rec_in, ret_in, new_id, new_rec, id_out, rec, ret, sem, parts):
    blk = ret.shape[2]
    width = rec.shape[1] // PARTS

    def part(k):
        return pl.ds(k * width, width)

    def load(k):
        return pltpu.make_async_copy(rec_in.at[:, part(k)], rec.at[:, part(k)], parts.at[k])

    def store(k):
        return pltpu.make_async_copy(rec.at[:, part(k)], new_rec.at[:, part(k)], parts.at[k])

    load_ret = pltpu.make_async_copy(ret_in, ret, sem.at[0])
    pass_on = pltpu.make_async_copy(new_id, id_out, sem.at[1])
    for k in range(PARTS):
        load(k).start()
    load_ret.start()
    pass_on.start()
    for k in range(PARTS):
        load(k).wait()
    load_ret.wait()
    shrink = 1.0 - RATE * DECAY

    @pl.loop(0, ret.shape[0])
    def _(s):
        cols = pl.ds(pl.multiple_of(send_list[s] * blk, blk), blk)
        rec[:, cols] = rec[:, cols] - (RATE / shrink) * ret[s].astype(F32)

    for k in range(PARTS):
        rec[:, part(k)] = rec[:, part(k)] * shrink
        store(k).start()
    for k in range(PARTS):
        store(k).wait()
    pass_on.wait()


def update(send_list, rec_t, ret, new_id):
    hbm = pl.BlockSpec(memory_space=pltpu.HBM)
    anywhere = pl.BlockSpec(memory_space=pl.ANY)
    dma = pltpu.SemaphoreType.DMA
    return pl.pallas_call(
        update_kernel,
        out_shape=(
            jax.ShapeDtypeStruct(rec_t.shape, F32),
            jax.ShapeDtypeStruct(new_id.shape, F32),
        ),
        in_specs=[pl.BlockSpec(memory_space=pltpu.SMEM)] + [anywhere] * 3,
        out_specs=(hbm, hbm),
        scratch_shapes=[
            pltpu.VMEM(rec_t.shape, F32),
            pltpu.VMEM(ret.shape, BF16),
            dma((2,)),
            dma((PARTS,)),
        ],
        compiler_params=pltpu.CompilerParams(vmem_limit_bytes=VMEM_BYTES),
        name="update",
    )(send_list, rec_t, ret, new_id)


def body(records, idents, rec_count, id_count, observed, send_list, slot_of_block, id_of_block):
    blk = observed.shape[1]
    wanted = send_list.reshape(-1)
    rec_t = records.T
    ret, new_id = exchange(
        wanted,
        slot_of_block,
        id_of_block,
        rec_count.reshape(-1, blk),
        id_count.reshape(-1, blk),
        rec_t,
        idents.T,
        observed,
    )
    new_rec, new_id = update(wanted, rec_t, ret, new_id)
    return new_rec.T, new_id.T


def solution(mesh):
    in_specs = (
        P("gx", "gy"),
        P("gx", "gy"),
        P("gx"),
        P("gx"),
        P("gx", None, None),
        P("gx", None),
        P("gx"),
        P("gx"),
    )
    out_specs = (P("gx", "gy"), P("gx", "gy"))
    return jax.shard_map(body, mesh=mesh, in_specs=in_specs, out_specs=out_specs, check_vma=False)
```

```python
import jax
import jax.numpy as jnp
from jax import lax
from jax.experimental import pallas as pl
from jax.experimental.pallas import tpu as pltpu
from jax.sharding import PartitionSpec as P

MESH = pl.DeviceIdType.MESH
RATE = 0.05
DECAY = 0.1
UNROLL = 8
GROUP = 4
PARTS = 4
VMEM_BYTES = 58 << 20
F32 = jnp.float32
BF16 = jnp.bfloat16


def dot_nn(a, b):
    return lax.dot_general(a, b, (((1,), (0,)), ((), ())), preferred_element_type=F32)


def dot_nt(a, b):
    return lax.dot_general(a, b, (((1,), (1,)), ((), ())), preferred_element_type=F32)


def log_weight(count):
    return jnp.log(1.0 + count.astype(F32)) / jnp.log(F32(1001.0))


def pairs_for(blocks, keys):
    return -(-(blocks + keys) // (2 * UNROLL)) * UNROLL


def column_of(row):
    size = row.shape[1]
    diagonal = lax.broadcasted_iota(jnp.int32, (size, size), 0) == lax.broadcasted_iota(
        jnp.int32, (size, size), 1
    )
    return jnp.sum(jnp.where(diagonal, row, 0.0), axis=1, keepdims=True)


def sorted_codes(key, payload, lanes):
    size = key.shape[1]
    across = lax.broadcasted_iota(jnp.int32, (size, size), 1)
    down = lax.broadcasted_iota(jnp.int32, (size, size), 0)
    key_col = column_of(key)
    equal = jnp.where(key == key_col, 1.0, 0.0)

    def places(count, earlier):
        odd = count - 2.0 * jnp.floor(0.5 * count)
        return 1.0 + jnp.where(earlier == 0.0, odd, 0.0)

    earlier = jnp.sum(jnp.where(across < down, equal, 0.0), axis=1, keepdims=True)
    places_col = places(jnp.sum(equal, axis=1, keepdims=True), earlier)
    earlier_row = jnp.sum(jnp.where(down < across, equal, 0.0), axis=0, keepdims=True)
    places_row = places(jnp.sum(equal, axis=0, keepdims=True), earlier_row)
    smaller = jnp.where(key < key_col, places_row, 0.0)
    rank = earlier + jnp.sum(smaller, axis=1, keepdims=True)
    marked = 2.0 * column_of(payload) + jnp.minimum(earlier, 1.0)
    value = lax.broadcasted_iota(jnp.int32, (1, lanes), 1).astype(F32)
    order = jnp.sum(jnp.where(rank == value, marked, 0.0), axis=0, keepdims=True)
    up_to = jnp.sum(jnp.where(key_col <= value, places_col, 0.0), axis=0, keepdims=True)
    used = jnp.sum(jnp.where(key_col == value, 1.0, 0.0), axis=0, keepdims=True)
    last = 2.0 * jnp.maximum(0.5 * up_to - 1.0, 0.0) + jnp.minimum(used, 1.0)
    return order.astype(jnp.int32), last.astype(jnp.int32)


def exchange_kernel(
    send_list, slot_row, id_row, rec_count, id_count,
    rec_hbm, id_hbm, obs_hbm,
    ret_out, new_id_out,
    rec, rec_bf, ids, new_ids, obs, w_rec, w_id, left, right, w_right, w_left, gram,
    left_send, weight_send, weight_got, back, ret, total, total_gram,
    plan, plan_smem, load_sem, ls, lr, ws, wr, fs, fr, bs, br, rs, rr,
):
    peers = lax.axis_size("gx")
    me = lax.axis_index("gx")
    half = lax.axis_index("gy")
    other = 1 - half
    idents = id_count.shape[0]
    blocks = obs.shape[0]
    blk = obs.shape[1]

    load_rec = pltpu.make_async_copy(rec_hbm, rec, load_sem.at[0])
    load_id = pltpu.make_async_copy(id_hbm, ids, load_sem.at[1])
    load_obs = pltpu.make_async_copy(obs_hbm, obs, load_sem.at[2])
    load_rec.start()
    load_id.start()
    barrier = pltpu.get_barrier_semaphore()

    @pl.loop(1, peers)
    def _(step):
        pl.semaphore_signal(
            barrier, inc=1, device_id={"gx": lax.rem(me + step, peers)}, device_id_type=MESH
        )

    pl.semaphore_signal(barrier, inc=1, device_id={"gy": other}, device_id_type=MESH)

    weights = log_weight(rec_count[...]).astype(BF16).astype(F32)
    for r in range(weights.shape[0]):
        w_rec[r] = weights[r : r + 1, :]

    def within(index, count):
        return jnp.clip(index, 0, count - 1)

    def column(block):
        return pl.ds(pl.multiple_of(block * blk, blk), blk)

    def unrolled(count, function):
        @pl.loop(0, count // GROUP)
        def _(i):
            for u in range(GROUP):
                function(i * GROUP + u)

    place = lax.broadcasted_iota(jnp.int32, (1, blocks), 1)
    code = ((place * 256 + slot_row[...] + 1) * 64 + id_row[...] + 1).astype(F32)
    for row, key in ((0, slot_row), (2, id_row)):
        order, last = sorted_codes(key[...].astype(F32), code, plan.shape[1])
        plan[row : row + 1, :] = order
        plan[row + 1 : row + 2, :] = last
    plan_copy = pltpu.make_async_copy(plan, plan_smem, load_sem.at[3])
    plan_copy.start()
    w_right[0] = jnp.zeros(w_right.shape[1:], BF16)
    w_left[0] = jnp.zeros(w_left.shape[1:], BF16)
    gram[0] = jnp.zeros(gram.shape[1:], F32)

    load_rec.wait()
    load_obs.start()

    def round_record(r):
        rec_bf[r] = rec[:, column(r)].astype(BF16)

    unrolled(rec_bf.shape[0], round_record)

    @pl.loop(0, peers)
    def _(peer):
        wanted = send_list[peer]
        left_send[peer] = rec_bf[wanted]
        weight_send[peer] = w_rec[wanted]

    left[half, me] = left_send[me]
    weight_got[me] = weight_send[me]
    pl.semaphore_wait(barrier, peers)

    def left_copy(peer, slot):
        return pltpu.make_async_remote_copy(
            src_ref=left_send.at[peer], dst_ref=left.at[half, slot],
            send_sem=ls.at[peer], recv_sem=lr.at[slot],
            device_id={"gx": peer}, device_id_type=MESH,
        )

    def weight_copy(peer, slot):
        return pltpu.make_async_remote_copy(
            src_ref=weight_send.at[peer], dst_ref=weight_got.at[slot],
            send_sem=ws.at[peer], recv_sem=wr.at[slot],
            device_id={"gx": peer}, device_id_type=MESH,
        )

    def forward_copy(slot, side):
        return pltpu.make_async_remote_copy(
            src_ref=left.at[side, slot], dst_ref=left.at[side, slot],
            send_sem=fs.at[slot], recv_sem=fr.at[slot],
            device_id={"gy": other}, device_id_type=MESH,
        )

    def back_copy(peer, slot):
        return pltpu.make_async_remote_copy(
            src_ref=back.at[peer], dst_ref=ret.at[slot],
            send_sem=bs.at[peer], recv_sem=br.at[slot],
            device_id={"gx": peer}, device_id_type=MESH,
        )

    def right_copy(side):
        return pltpu.make_async_remote_copy(
            src_ref=right.at[side], dst_ref=right.at[side],
            send_sem=rs, recv_sem=rr,
            device_id={"gy": other}, device_id_type=MESH,
        )

    @pl.loop(1, peers)
    def _(step):
        peer = lax.rem(me + step, peers)
        left_copy(peer, me).start()
        weight_copy(peer, me).start()

    forward_copy(me, half).start()
    load_id.wait()
    w_id[...] = log_weight(id_count[...])

    def round_ident(c):
        rows = ids[:, column(c)].astype(BF16)
        right[half, c] = rows
        w_right[c + 1] = (rows.astype(F32) * w_id[pl.ds(c, 1), :]).astype(BF16)

    unrolled(idents, round_ident)
    right_copy(half).start()

    right_copy(other).wait_recv()

    def full_right(c):
        return jnp.concatenate([right[0, c], right[1, c]], axis=0)

    def full_left(s):
        return jnp.concatenate([left[0, s], left[1, s]], axis=0)

    def right_gram(c):
        gram[c + 1] = dot_nt(w_right[c + 1], full_right(c))

    unrolled(idents, right_gram)
    load_obs.wait()
    plan_copy.wait()

    def running_sums(row, pairs, term):
        def one(place):
            code = plan_smem[row, place]
            return within(code >> 15, blocks), within((code >> 7) & 255, peers + 1), within(
                (code >> 1) & 63, idents + 1
            )

        def step(i, carry):
            acc, acc_gram = carry
            for u in range(UNROLL):
                p = i * UNROLL + u
                keep = (plan_smem[row, 2 * p] & 1).astype(F32)
                product, matrix = term(one(2 * p), one(2 * p + 1))
                acc = acc * keep + product
                acc_gram = acc_gram * keep + matrix
                total[p] = acc
                total_gram[p] = acc_gram
            return acc, acc_gram

        zero = jnp.zeros(total.shape[1:], F32)
        lax.fori_loop(0, pairs // UNROLL, step, (zero, zero))

    def slot_term(first, second):
        (b0, _, c0), (b1, _, c1) = first, second
        factors = jnp.concatenate([w_right[c0], w_right[c1]], axis=1)
        values = jnp.concatenate([obs[b0], obs[b1]], axis=1)
        return dot_nt(factors, values), gram[c0] + gram[c1]

    def id_term(first, second):
        (b0, s0, _), (b1, s1, _) = first, second
        factors = jnp.concatenate([w_left[s0], w_left[s1]], axis=1)
        values = jnp.concatenate([obs[b0], obs[b1]], axis=0)
        return dot_nn(factors, values), gram[s0] + gram[s1]

    running_sums(0, pairs_for(blocks, peers), slot_term)

    def finish_slot(s):
        last = within(plan_smem[1, s] >> 1, total.shape[0])
        score = dot_nn(total_gram[last].astype(BF16), full_left(s))
        back[s] = ((score - total[last]) * weight_got[s]).astype(BF16)

    def left_factors(s):
        rows = (left[half, s].astype(F32) * weight_got[s]).astype(BF16)
        w_left[s + 1] = rows
        gram[s + 1] = dot_nt(rows, full_left(s))

    @pl.loop(1, peers)
    def _(step):
        source = lax.rem(me - step + peers, peers)
        left_copy(source, source).wait_recv()
        weight_copy(source, source).wait_recv()
        forward_copy(source, half).start()

    @pl.loop(0, peers // GROUP)
    def _(i):
        sources = [lax.rem(me - (i * GROUP + u) + peers, peers) for u in range(GROUP)]
        for source in sources:
            forward_copy(source, other).wait_recv()
        for source in sources:
            finish_slot(source)
        for u, source in enumerate(sources):
            if u > 0:
                back_copy(source, me).start()
            else:

                @pl.when(i > 0)
                def _():
                    back_copy(source, me).start()

    ret[me] = back[me]
    unrolled(peers, left_factors)
    running_sums(2, pairs_for(blocks, idents), id_term)

    def finish_ident(c):
        at = within(plan_smem[3, c] >> 1, total.shape[0])
        used = (plan_smem[3, c] & 1).astype(F32)
        score = dot_nn(total_gram[at].astype(BF16), full_right(c))
        grad = (score - total[at]) * (w_id[pl.ds(c, 1), :] * used)
        old = ids[:, column(c)]
        new_ids[:, column(c)] = old - RATE * (grad + DECAY * old)

    unrolled(idents, finish_ident)
    store_id = pltpu.make_async_copy(new_ids, new_id_out, load_sem.at[1])
    store_id.start()

    @pl.loop(1, peers)
    def _(step):
        source = lax.rem(me - step + peers, peers)
        back_copy(source, source).wait_recv()

    store_ret = pltpu.make_async_copy(ret, ret_out, load_sem.at[0])
    store_ret.start()

    right_copy(half).wait_send()
    forward_copy(me, half).wait_send()

    @pl.loop(1, peers)
    def _(step):
        peer = lax.rem(me + step, peers)
        left_copy(peer, me).wait_send()
        weight_copy(peer, me).wait_send()
        forward_copy(peer, half).wait_send()
        back_copy(peer, me).wait_send()

    store_id.wait()
    store_ret.wait()


def exchange(send_list, slot_of_block, id_of_block, rec_count, id_count, rec_t, id_t, obs):
    peers = lax.axis_size("gx")
    half_cols = rec_t.shape[0]
    blocks, blk, _ = obs.shape
    idents = id_count.shape[0]
    pairs = pairs_for(blocks, max(peers, idents))
    lanes = -(-2 * pairs // 128) * 128
    smem = pl.BlockSpec(memory_space=pltpu.SMEM)
    vmem = pl.BlockSpec(memory_space=pltpu.VMEM)
    hbm = pl.BlockSpec(memory_space=pltpu.HBM)
    anywhere = pl.BlockSpec(memory_space=pl.ANY)
    dma = pltpu.SemaphoreType.DMA
    return pl.pallas_call(
        exchange_kernel,
        out_shape=(
            jax.ShapeDtypeStruct((peers, half_cols, blk), BF16),
            jax.ShapeDtypeStruct(id_t.shape, F32),
        ),
        in_specs=[smem] + [vmem] * 4 + [hbm] * 3,
        out_specs=(anywhere, anywhere),
        scratch_shapes=[
            pltpu.VMEM(rec_t.shape, F32),
            pltpu.VMEM((rec_count.shape[0], half_cols, blk), BF16),
            pltpu.VMEM(id_t.shape, F32),
            pltpu.VMEM(id_t.shape, F32),
            pltpu.VMEM(obs.shape, BF16),
            pltpu.VMEM((rec_count.shape[0], 1, blk), F32),
            pltpu.VMEM(id_count.shape, F32),
            pltpu.VMEM((2, peers, half_cols, blk), BF16),
            pltpu.VMEM((2, idents, half_cols, blk), BF16),
            pltpu.VMEM((idents + 1, half_cols, blk), BF16),
            pltpu.VMEM((peers + 1, half_cols, blk), BF16),
            pltpu.VMEM((max(idents, peers) + 1, half_cols, 2 * half_cols), F32),
            pltpu.VMEM((peers, half_cols, blk), BF16),
            pltpu.VMEM((peers, 1, blk), F32),
            pltpu.VMEM((peers, 1, blk), F32),
            pltpu.VMEM((peers, half_cols, blk), BF16),
            pltpu.VMEM((peers, half_cols, blk), BF16),
            pltpu.VMEM((pairs, half_cols, blk), F32),
            pltpu.VMEM((pairs, half_cols, 2 * half_cols), F32),
            pltpu.VMEM((8, lanes), jnp.int32),
            pltpu.SMEM((8, lanes), jnp.int32),
            dma((4,)),
        ]
        + [dma((peers,))] * 8
        + [dma, dma],
        compiler_params=pltpu.CompilerParams(
            collective_id=0, has_side_effects=True, vmem_limit_bytes=VMEM_BYTES
        ),
        name="exchange",
    )(
        send_list, slot_of_block[None], id_of_block[None],
        rec_count, id_count, rec_t, id_t, obs,
    )


def update_kernel(
    send_list, rec_in, ret_in, new_id, new_rec, id_out, rec, ret, ids, sem, parts
):
    blk = ret.shape[2]
    width = rec.shape[1] // PARTS

    def part(k):
        return pl.ds(k * width, width)

    def load(k):
        return pltpu.make_async_copy(rec_in.at[:, part(k)], rec.at[:, part(k)], parts.at[k])

    def store(k):
        return pltpu.make_async_copy(rec.at[:, part(k)], new_rec.at[:, part(k)], parts.at[k])

    load_ret = pltpu.make_async_copy(ret_in, ret, sem.at[0])
    load_id = pltpu.make_async_copy(new_id, ids, sem.at[1])
    store_id = pltpu.make_async_copy(ids, id_out, sem.at[1])
    for k in range(PARTS):
        load(k).start()
    load_ret.start()
    load_id.start()
    for k in range(PARTS):
        load(k).wait()
    load_ret.wait()
    load_id.wait()
    store_id.start()
    shrink = 1.0 - RATE * DECAY

    @pl.loop(0, ret.shape[0])
    def _(s):
        cols = pl.ds(pl.multiple_of(send_list[s] * blk, blk), blk)
        rec[:, cols] = rec[:, cols] - (RATE / shrink) * ret[s].astype(F32)

    for k in range(PARTS):
        rec[:, part(k)] = rec[:, part(k)] * shrink
        store(k).start()
    for k in range(PARTS):
        store(k).wait()
    store_id.wait()


def update(send_list, rec_t, ret, new_id):
    hbm = pl.BlockSpec(memory_space=pltpu.HBM)
    anywhere = pl.BlockSpec(memory_space=pl.ANY)
    dma = pltpu.SemaphoreType.DMA
    return pl.pallas_call(
        update_kernel,
        out_shape=(
            jax.ShapeDtypeStruct(rec_t.shape, F32),
            jax.ShapeDtypeStruct(new_id.shape, F32),
        ),
        in_specs=[pl.BlockSpec(memory_space=pltpu.SMEM)] + [anywhere] * 3,
        out_specs=(hbm, hbm),
        scratch_shapes=[
            pltpu.VMEM(rec_t.shape, F32),
            pltpu.VMEM(ret.shape, BF16),
            pltpu.VMEM(new_id.shape, F32),
            dma((2,)),
            dma((PARTS,)),
        ],
        compiler_params=pltpu.CompilerParams(vmem_limit_bytes=VMEM_BYTES),
        name="update",
    )(send_list, rec_t, ret, new_id)


def body(records, idents, rec_count, id_count, observed, send_list, slot_of_block, id_of_block):
    blk = observed.shape[1]
    wanted = send_list.reshape(-1)
    rec_t = records.T
    ret, new_id = exchange(
        wanted,
        slot_of_block,
        id_of_block,
        rec_count.reshape(-1, blk),
        id_count.reshape(-1, blk),
        rec_t,
        idents.T,
        observed,
    )
    new_rec, new_id = update(wanted, rec_t, ret, new_id)
    return new_rec.T, new_id.T


def solution(mesh):
    in_specs = (
        P("gx", "gy"),
        P("gx", "gy"),
        P("gx"),
        P("gx"),
        P("gx", None, None),
        P("gx", None),
        P("gx"),
        P("gx"),
    )
    out_specs = (P("gx", "gy"), P("gx", "gy"))
    return jax.shard_map(body, mesh=mesh, in_specs=in_specs, out_specs=out_specs, check_vma=False)
```

```python
import jax
import jax.numpy as jnp
from jax import lax
from jax.experimental import pallas as pl
from jax.experimental.pallas import tpu as pltpu
from jax.sharding import PartitionSpec as P

MESH = pl.DeviceIdType.MESH
RATE = 0.05
DECAY = 0.1
UNROLL = 8
GROUP = 4
PARTS = 4
VMEM_BYTES = 58 << 20
F32 = jnp.float32
BF16 = jnp.bfloat16


def dot_nn(a, b):
    return lax.dot_general(a, b, (((1,), (0,)), ((), ())), preferred_element_type=F32)


def dot_nt(a, b):
    return lax.dot_general(a, b, (((1,), (1,)), ((), ())), preferred_element_type=F32)


def log_weight(count):
    return jnp.log(1.0 + count.astype(F32)) / jnp.log(F32(1001.0))


def pairs_for(blocks, keys):
    return -(-(blocks + keys) // (2 * UNROLL)) * UNROLL


def column_of(row):
    size = row.shape[1]
    diagonal = lax.broadcasted_iota(jnp.int32, (size, size), 0) == lax.broadcasted_iota(
        jnp.int32, (size, size), 1
    )
    return jnp.sum(jnp.where(diagonal, row, 0.0), axis=1, keepdims=True)


def sorted_codes(key, payload, lanes):
    size = key.shape[1]
    across = lax.broadcasted_iota(jnp.int32, (size, size), 1)
    down = lax.broadcasted_iota(jnp.int32, (size, size), 0)
    key_col = column_of(key)
    equal = jnp.where(key == key_col, 1.0, 0.0)

    def places(count, earlier):
        odd = count - 2.0 * jnp.floor(0.5 * count)
        return 1.0 + jnp.where(earlier == 0.0, odd, 0.0)

    earlier = jnp.sum(jnp.where(across < down, equal, 0.0), axis=1, keepdims=True)
    places_col = places(jnp.sum(equal, axis=1, keepdims=True), earlier)
    earlier_row = jnp.sum(jnp.where(down < across, equal, 0.0), axis=0, keepdims=True)
    places_row = places(jnp.sum(equal, axis=0, keepdims=True), earlier_row)
    smaller = jnp.where(key < key_col, places_row, 0.0)
    rank = earlier + jnp.sum(smaller, axis=1, keepdims=True)
    marked = 2.0 * column_of(payload) + jnp.minimum(earlier, 1.0)
    value = lax.broadcasted_iota(jnp.int32, (1, lanes), 1).astype(F32)
    order = jnp.sum(jnp.where(rank == value, marked, 0.0), axis=0, keepdims=True)
    up_to = jnp.sum(jnp.where(key_col <= value, places_col, 0.0), axis=0, keepdims=True)
    used = jnp.sum(jnp.where(key_col == value, 1.0, 0.0), axis=0, keepdims=True)
    last = 2.0 * jnp.maximum(0.5 * up_to - 1.0, 0.0) + jnp.minimum(used, 1.0)
    return order.astype(jnp.int32), last.astype(jnp.int32)


def exchange_kernel(
    send_list, slot_row, id_row, rec_count, id_count,
    rec_hbm, id_hbm, obs_hbm,
    ret_out, new_id_out,
    rec, rec_bf, ids, new_ids, obs, w_rec, w_id, left, right, w_right, w_left, gram,
    left_send, weight_send, weight_got, back, ret, total, total_gram,
    plan, plan_smem, load_sem, ls, lr, ws, wr, fs, fr, bs, br, rs, rr,
):
    peers = lax.axis_size("gx")
    me = lax.axis_index("gx")
    half = lax.axis_index("gy")
    other = 1 - half
    idents = id_count.shape[0]
    blocks = obs.shape[0]
    blk = obs.shape[1]

    load_rec = pltpu.make_async_copy(rec_hbm, rec, load_sem.at[0])
    load_id = pltpu.make_async_copy(id_hbm, ids, load_sem.at[1])
    load_obs = pltpu.make_async_copy(obs_hbm, obs, load_sem.at[2])
    load_rec.start()
    load_id.start()
    barrier = pltpu.get_barrier_semaphore()

    @pl.loop(1, peers)
    def _(step):
        pl.semaphore_signal(
            barrier, inc=1, device_id={"gx": lax.rem(me + step, peers)}, device_id_type=MESH
        )

    pl.semaphore_signal(barrier, inc=1, device_id={"gy": other}, device_id_type=MESH)

    weights = log_weight(rec_count[...]).astype(BF16).astype(F32)
    for r in range(weights.shape[0]):
        w_rec[r] = weights[r : r + 1, :]

    def within(index, count):
        return jnp.clip(index, 0, count - 1)

    def column(block):
        return pl.ds(pl.multiple_of(block * blk, blk), blk)

    def unrolled(count, function):
        @pl.loop(0, count // GROUP)
        def _(i):
            for u in range(GROUP):
                function(i * GROUP + u)

    load_rec.wait()
    load_obs.start()

    def round_record(r):
        rec_bf[r] = rec[:, column(r)].astype(BF16)

    unrolled(rec_bf.shape[0], round_record)

    @pl.loop(0, peers)
    def _(peer):
        wanted = send_list[peer]
        left_send[peer] = rec_bf[wanted]
        weight_send[peer] = w_rec[wanted]

    left[half, me] = left_send[me]
    weight_got[me] = weight_send[me]
    pl.semaphore_wait(barrier, peers)

    def left_copy(peer, slot):
        return pltpu.make_async_remote_copy(
            src_ref=left_send.at[peer], dst_ref=left.at[half, slot],
            send_sem=ls.at[peer], recv_sem=lr.at[slot],
            device_id={"gx": peer}, device_id_type=MESH,
        )

    def weight_copy(peer, slot):
        return pltpu.make_async_remote_copy(
            src_ref=weight_send.at[peer], dst_ref=weight_got.at[slot],
            send_sem=ws.at[peer], recv_sem=wr.at[slot],
            device_id={"gx": peer}, device_id_type=MESH,
        )

    def forward_copy(slot, side):
        return pltpu.make_async_remote_copy(
            src_ref=left.at[side, slot], dst_ref=left.at[side, slot],
            send_sem=fs.at[slot], recv_sem=fr.at[slot],
            device_id={"gy": other}, device_id_type=MESH,
        )

    def back_copy(peer, slot):
        return pltpu.make_async_remote_copy(
            src_ref=back.at[peer], dst_ref=ret.at[slot],
            send_sem=bs.at[peer], recv_sem=br.at[slot],
            device_id={"gx": peer}, device_id_type=MESH,
        )

    def right_copy(side):
        return pltpu.make_async_remote_copy(
            src_ref=right.at[side], dst_ref=right.at[side],
            send_sem=rs, recv_sem=rr,
            device_id={"gy": other}, device_id_type=MESH,
        )

    @pl.loop(1, peers)
    def _(step):
        peer = lax.rem(me + step, peers)
        left_copy(peer, me).start()
        weight_copy(peer, me).start()

    forward_copy(me, half).start()
    load_id.wait()
    w_id[...] = log_weight(id_count[...])

    def round_ident(c):
        rows = ids[:, column(c)].astype(BF16)
        right[half, c] = rows
        w_right[c + 1] = (rows.astype(F32) * w_id[pl.ds(c, 1), :]).astype(BF16)

    unrolled(idents, round_ident)
    right_copy(half).start()

    place = lax.broadcasted_iota(jnp.int32, (1, blocks), 1)
    code = ((place * 256 + slot_row[...] + 1) * 64 + id_row[...] + 1).astype(F32)

    def sort_by(which, key):
        order, last = sorted_codes(key[...].astype(F32), code, plan.shape[2])
        plan[which, 0:1, :] = order
        plan[which, 1:2, :] = last
        copy = pltpu.make_async_copy(plan.at[which], plan_smem.at[which], load_sem.at[3 + which])
        copy.start()
        return copy

    slot_plan = sort_by(0, slot_row)
    w_right[0] = jnp.zeros(w_right.shape[1:], BF16)
    w_left[0] = jnp.zeros(w_left.shape[1:], BF16)
    gram[0] = jnp.zeros(gram.shape[1:], F32)

    def full_right(c):
        return jnp.concatenate([right[0, c], right[1, c]], axis=0)

    def full_left(s):
        return jnp.concatenate([left[0, s], left[1, s]], axis=0)

    def right_gram(c):
        gram[c + 1] = dot_nt(w_right[c + 1], full_right(c))


    def running_sums(which, pairs, terms, sums):
        def one(place):
            code = plan_smem[which, 0, place]
            return within(code >> 15, blocks), within((code >> 7) & 255, peers + 1), within(
                (code >> 1) & 63, idents + 1
            )

        def step(i, carry):
            for u in range(UNROLL):
                p = i * UNROLL + u
                keep = (plan_smem[which, 0, 2 * p] & 1).astype(F32)
                new = terms(one(2 * p), one(2 * p + 1))
                carry = tuple(acc * keep + term for acc, term in zip(carry, new))
                for ref, acc in zip(sums, carry):
                    ref[p] = acc
            return carry

        zero = tuple(jnp.zeros(ref.shape[1:], F32) for ref in sums)
        lax.fori_loop(0, pairs // UNROLL, step, zero)

    def slot_product(first, second):
        (b0, _, c0), (b1, _, c1) = first, second
        factors = jnp.concatenate([w_right[c0], w_right[c1]], axis=1)
        values = jnp.concatenate([obs[b0], obs[b1]], axis=1)
        return (dot_nt(factors, values),)

    def slot_gram(first, second):
        return (gram[first[2]] + gram[second[2]],)

    def id_terms(first, second):
        (b0, s0, _), (b1, s1, _) = first, second
        factors = jnp.concatenate([w_left[s0], w_left[s1]], axis=1)
        values = jnp.concatenate([obs[b0], obs[b1]], axis=0)
        return dot_nn(factors, values), gram[s0] + gram[s1]

    slot_plan.wait()
    load_obs.wait()
    running_sums(0, pairs_for(blocks, peers), slot_product, (total,))
    right_copy(other).wait_recv()
    unrolled(idents, right_gram)

    @pl.loop(1, peers)
    def _(step):
        source = lax.rem(me - step + peers, peers)
        left_copy(source, source).wait_recv()
        weight_copy(source, source).wait_recv()
        forward_copy(source, half).start()

    running_sums(0, pairs_for(blocks, peers), slot_gram, (total_gram,))

    def finish_slot(s):
        last = within(plan_smem[0, 1, s] >> 1, total.shape[0])
        score = dot_nn(total_gram[last].astype(BF16), full_left(s))
        back[s] = ((score - total[last]) * weight_got[s]).astype(BF16)

    def left_factors(s):
        rows = (left[half, s].astype(F32) * weight_got[s]).astype(BF16)
        w_left[s + 1] = rows
        gram[s + 1] = dot_nt(rows, full_left(s))

    @pl.loop(0, peers // GROUP)
    def _(i):
        sources = [lax.rem(me - (i * GROUP + u) + peers, peers) for u in range(GROUP)]
        for source in sources:
            forward_copy(source, other).wait_recv()
        for source in sources:
            finish_slot(source)
        for u, source in enumerate(sources):
            if u > 0:
                back_copy(source, me).start()
            else:

                @pl.when(i > 0)
                def _():
                    back_copy(source, me).start()

    id_plan = sort_by(1, id_row)
    ret[me] = back[me]
    unrolled(peers, left_factors)
    id_plan.wait()
    running_sums(1, pairs_for(blocks, idents), id_terms, (total, total_gram))

    def finish_ident(c):
        at = within(plan_smem[1, 1, c] >> 1, total.shape[0])
        used = (plan_smem[1, 1, c] & 1).astype(F32)
        score = dot_nn(total_gram[at].astype(BF16), full_right(c))
        grad = (score - total[at]) * (w_id[pl.ds(c, 1), :] * used)
        old = ids[:, column(c)]
        new_ids[:, column(c)] = old - RATE * (grad + DECAY * old)

    unrolled(idents, finish_ident)
    store_id = pltpu.make_async_copy(new_ids, new_id_out, load_sem.at[1])
    store_id.start()

    @pl.loop(1, peers)
    def _(step):
        source = lax.rem(me - step + peers, peers)
        back_copy(source, source).wait_recv()

    store_ret = pltpu.make_async_copy(ret, ret_out, load_sem.at[0])
    store_ret.start()

    right_copy(half).wait_send()
    forward_copy(me, half).wait_send()

    @pl.loop(1, peers)
    def _(step):
        peer = lax.rem(me + step, peers)
        left_copy(peer, me).wait_send()
        weight_copy(peer, me).wait_send()
        forward_copy(peer, half).wait_send()
        back_copy(peer, me).wait_send()

    store_id.wait()
    store_ret.wait()


def exchange(send_list, slot_of_block, id_of_block, rec_count, id_count, rec_t, id_t, obs):
    peers = lax.axis_size("gx")
    half_cols = rec_t.shape[0]
    blocks, blk, _ = obs.shape
    idents = id_count.shape[0]
    pairs = pairs_for(blocks, max(peers, idents))
    lanes = -(-2 * pairs // 128) * 128
    smem = pl.BlockSpec(memory_space=pltpu.SMEM)
    vmem = pl.BlockSpec(memory_space=pltpu.VMEM)
    hbm = pl.BlockSpec(memory_space=pltpu.HBM)
    anywhere = pl.BlockSpec(memory_space=pl.ANY)
    dma = pltpu.SemaphoreType.DMA
    return pl.pallas_call(
        exchange_kernel,
        out_shape=(
            jax.ShapeDtypeStruct((peers, half_cols, blk), BF16),
            jax.ShapeDtypeStruct(id_t.shape, F32),
        ),
        in_specs=[smem] + [vmem] * 4 + [hbm] * 3,
        out_specs=(anywhere, anywhere),
        scratch_shapes=[
            pltpu.VMEM(rec_t.shape, F32),
            pltpu.VMEM((rec_count.shape[0], half_cols, blk), BF16),
            pltpu.VMEM(id_t.shape, F32),
            pltpu.VMEM(id_t.shape, F32),
            pltpu.VMEM(obs.shape, BF16),
            pltpu.VMEM((rec_count.shape[0], 1, blk), F32),
            pltpu.VMEM(id_count.shape, F32),
            pltpu.VMEM((2, peers, half_cols, blk), BF16),
            pltpu.VMEM((2, idents, half_cols, blk), BF16),
            pltpu.VMEM((idents + 1, half_cols, blk), BF16),
            pltpu.VMEM((peers + 1, half_cols, blk), BF16),
            pltpu.VMEM((max(idents, peers) + 1, half_cols, 2 * half_cols), F32),
            pltpu.VMEM((peers, half_cols, blk), BF16),
            pltpu.VMEM((peers, 1, blk), F32),
            pltpu.VMEM((peers, 1, blk), F32),
            pltpu.VMEM((peers, half_cols, blk), BF16),
            pltpu.VMEM((peers, half_cols, blk), BF16),
            pltpu.VMEM((pairs, half_cols, blk), F32),
            pltpu.VMEM((pairs, half_cols, 2 * half_cols), F32),
            pltpu.VMEM((2, 8, lanes), jnp.int32),
            pltpu.SMEM((2, 8, lanes), jnp.int32),
            dma((5,)),
        ]
        + [dma((peers,))] * 8
        + [dma, dma],
        compiler_params=pltpu.CompilerParams(
            collective_id=0, has_side_effects=True, vmem_limit_bytes=VMEM_BYTES
        ),
        name="exchange",
    )(
        send_list, slot_of_block[None], id_of_block[None],
        rec_count, id_count, rec_t, id_t, obs,
    )


def update_kernel(
    send_list, rec_in, ret_in, new_id, new_rec, id_out, rec, ret, ids, sem, parts
):
    blk = ret.shape[2]
    width = rec.shape[1] // PARTS

    def part(k):
        return pl.ds(k * width, width)

    def load(k):
        return pltpu.make_async_copy(rec_in.at[:, part(k)], rec.at[:, part(k)], parts.at[k])

    def store(k):
        return pltpu.make_async_copy(rec.at[:, part(k)], new_rec.at[:, part(k)], parts.at[k])

    load_ret = pltpu.make_async_copy(ret_in, ret, sem.at[0])
    load_id = pltpu.make_async_copy(new_id, ids, sem.at[1])
    store_id = pltpu.make_async_copy(ids, id_out, sem.at[1])
    for k in range(PARTS):
        load(k).start()
    load_ret.start()
    load_id.start()
    shrink = 1.0 - RATE * DECAY
    for k in range(PARTS):
        load(k).wait()
        rec[:, part(k)] = rec[:, part(k)] * shrink
    load_ret.wait()

    @pl.loop(0, ret.shape[0])
    def _(s):
        cols = pl.ds(pl.multiple_of(send_list[s] * blk, blk), blk)
        rec[:, cols] = rec[:, cols] - RATE * ret[s].astype(F32)

    for k in range(PARTS):
        store(k).start()
    load_id.wait()
    store_id.start()
    for k in range(PARTS):
        store(k).wait()
    store_id.wait()


def update(send_list, rec_t, ret, new_id):
    hbm = pl.BlockSpec(memory_space=pltpu.HBM)
    anywhere = pl.BlockSpec(memory_space=pl.ANY)
    dma = pltpu.SemaphoreType.DMA
    return pl.pallas_call(
        update_kernel,
        out_shape=(
            jax.ShapeDtypeStruct(rec_t.shape, F32),
            jax.ShapeDtypeStruct(new_id.shape, F32),
        ),
        in_specs=[pl.BlockSpec(memory_space=pltpu.SMEM)] + [anywhere] * 3,
        out_specs=(hbm, hbm),
        scratch_shapes=[
            pltpu.VMEM(rec_t.shape, F32),
            pltpu.VMEM(ret.shape, BF16),
            pltpu.VMEM(new_id.shape, F32),
            dma((2,)),
            dma((PARTS,)),
        ],
        compiler_params=pltpu.CompilerParams(vmem_limit_bytes=VMEM_BYTES),
        name="update",
    )(send_list, rec_t, ret, new_id)


def body(records, idents, rec_count, id_count, observed, send_list, slot_of_block, id_of_block):
    blk = observed.shape[1]
    wanted = send_list.reshape(-1)
    rec_t = records.T
    ret, new_id = exchange(
        wanted,
        slot_of_block,
        id_of_block,
        rec_count.reshape(-1, blk),
        id_count.reshape(-1, blk),
        rec_t,
        idents.T,
        observed,
    )
    new_rec, new_id = update(wanted, rec_t, ret, new_id)
    return new_rec.T, new_id.T


def solution(mesh):
    in_specs = (
        P("gx", "gy"),
        P("gx", "gy"),
        P("gx"),
        P("gx"),
        P("gx", None, None),
        P("gx", None),
        P("gx"),
        P("gx"),
    )
    out_specs = (P("gx", "gy"), P("gx", "gy"))
    return jax.shard_map(body, mesh=mesh, in_specs=in_specs, out_specs=out_specs, check_vma=False)
```

```python
import jax
import jax.numpy as jnp
from jax import lax
from jax.experimental import pallas as pl
from jax.experimental.pallas import tpu as pltpu
from jax.sharding import PartitionSpec as P

MESH = pl.DeviceIdType.MESH
RATE = 0.05
DECAY = 0.1
UNROLL = 8
GROUP = 8
ROUNDS = 4
PARTS = 4
VMEM_BYTES = 58 << 20
F32 = jnp.float32
BF16 = jnp.bfloat16


def dot_nn(a, b):
    return lax.dot_general(a, b, (((1,), (0,)), ((), ())), preferred_element_type=F32)


def dot_nt(a, b):
    return lax.dot_general(a, b, (((1,), (1,)), ((), ())), preferred_element_type=F32)


def log_weight(count):
    return jnp.log(1.0 + count.astype(F32)) / jnp.log(F32(1001.0))


def pairs_for(blocks, keys):
    return -(-(blocks + keys) // (2 * UNROLL)) * UNROLL


def column_of(row):
    size = row.shape[1]
    diagonal = lax.broadcasted_iota(jnp.int32, (size, size), 0) == lax.broadcasted_iota(
        jnp.int32, (size, size), 1
    )
    return jnp.sum(jnp.where(diagonal, row, 0.0), axis=1, keepdims=True)


def sorted_codes(key, payload, lanes):
    size = key.shape[1]
    across = lax.broadcasted_iota(jnp.int32, (size, size), 1)
    down = lax.broadcasted_iota(jnp.int32, (size, size), 0)
    key_col = column_of(key)
    equal = jnp.where(key == key_col, 1.0, 0.0)

    def places(count, earlier):
        odd = count - 2.0 * jnp.floor(0.5 * count)
        return 1.0 + jnp.where(earlier == 0.0, odd, 0.0)

    earlier = jnp.sum(jnp.where(across < down, equal, 0.0), axis=1, keepdims=True)
    places_col = places(jnp.sum(equal, axis=1, keepdims=True), earlier)
    earlier_row = jnp.sum(jnp.where(down < across, equal, 0.0), axis=0, keepdims=True)
    places_row = places(jnp.sum(equal, axis=0, keepdims=True), earlier_row)
    smaller = jnp.where(key < key_col, places_row, 0.0)
    rank = earlier + jnp.sum(smaller, axis=1, keepdims=True)
    marked = 2.0 * column_of(payload) + jnp.minimum(earlier, 1.0)
    value = lax.broadcasted_iota(jnp.int32, (1, lanes), 1).astype(F32)
    order = jnp.sum(jnp.where(rank == value, marked, 0.0), axis=0, keepdims=True)
    up_to = jnp.sum(jnp.where(key_col <= value, places_col, 0.0), axis=0, keepdims=True)
    used = jnp.sum(jnp.where(key_col == value, 1.0, 0.0), axis=0, keepdims=True)
    last = 2.0 * jnp.maximum(0.5 * up_to - 1.0, 0.0) + jnp.minimum(used, 1.0)
    return order.astype(jnp.int32), last.astype(jnp.int32)


def exchange_kernel(
    send_list, slot_row, id_row, rec_count, id_count,
    rec_hbm, id_hbm, obs_hbm,
    ret_out, new_id_out,
    rec, rec_bf, ids, new_ids, obs, w_rec, w_id, left, right, w_right, w_left, gram,
    left_send, weight_send, weight_got, back, ret, total, total_gram,
    plan, plan_smem, load_sem, ls, lr, ws, wr, fs, fr, bs, br, rs, rr,
):
    peers = lax.axis_size("gx")
    me = lax.axis_index("gx")
    half = lax.axis_index("gy")
    other = 1 - half
    idents = id_count.shape[0]
    blocks = obs.shape[0]
    blk = obs.shape[1]

    load_rec = pltpu.make_async_copy(rec_hbm, rec, load_sem.at[0])
    load_id = pltpu.make_async_copy(id_hbm, ids, load_sem.at[1])
    load_obs = pltpu.make_async_copy(obs_hbm, obs, load_sem.at[2])
    load_rec.start()
    load_id.start()
    barrier = pltpu.get_barrier_semaphore()

    @pl.loop(1, peers)
    def _(step):
        pl.semaphore_signal(
            barrier, inc=1, device_id={"gx": lax.rem(me + step, peers)}, device_id_type=MESH
        )

    pl.semaphore_signal(barrier, inc=1, device_id={"gy": other}, device_id_type=MESH)

    weights = log_weight(rec_count[...]).astype(BF16).astype(F32)
    for r in range(weights.shape[0]):
        w_rec[r] = weights[r : r + 1, :]

    def within(index, count):
        return jnp.clip(index, 0, count - 1)

    def column(block):
        return pl.ds(pl.multiple_of(block * blk, blk), blk)

    def unrolled(count, function):
        @pl.loop(0, count // GROUP)
        def _(i):
            for u in range(GROUP):
                function(i * GROUP + u)

    load_rec.wait()
    load_obs.start()

    def round_record(r):
        rec_bf[r] = rec[:, column(r)].astype(BF16)

    unrolled(rec_bf.shape[0], round_record)

    @pl.loop(0, peers)
    def _(peer):
        wanted = send_list[peer]
        left_send[peer] = rec_bf[wanted]
        weight_send[peer] = w_rec[wanted]

    left[half, me] = left_send[me]
    weight_got[me] = weight_send[me]
    pl.semaphore_wait(barrier, peers)

    def left_copy(peer, slot):
        return pltpu.make_async_remote_copy(
            src_ref=left_send.at[peer], dst_ref=left.at[half, slot],
            send_sem=ls.at[peer], recv_sem=lr.at[slot],
            device_id={"gx": peer}, device_id_type=MESH,
        )

    def weight_copy(peer, slot):
        return pltpu.make_async_remote_copy(
            src_ref=weight_send.at[peer], dst_ref=weight_got.at[slot],
            send_sem=ws.at[peer], recv_sem=wr.at[slot],
            device_id={"gx": peer}, device_id_type=MESH,
        )

    def forward_copy(slot, side):
        return pltpu.make_async_remote_copy(
            src_ref=left.at[side, slot], dst_ref=left.at[side, slot],
            send_sem=fs.at[slot], recv_sem=fr.at[slot],
            device_id={"gy": other}, device_id_type=MESH,
        )

    def back_copy(peer, slot):
        return pltpu.make_async_remote_copy(
            src_ref=back.at[peer], dst_ref=ret.at[slot],
            send_sem=bs.at[peer], recv_sem=br.at[slot],
            device_id={"gx": peer}, device_id_type=MESH,
        )

    def right_copy(side):
        return pltpu.make_async_remote_copy(
            src_ref=right.at[side], dst_ref=right.at[side],
            send_sem=rs, recv_sem=rr,
            device_id={"gy": other}, device_id_type=MESH,
        )

    @pl.loop(1, peers)
    def _(step):
        peer = lax.rem(me + step, peers)
        left_copy(peer, me).start()
        weight_copy(peer, me).start()

    forward_copy(me, half).start()
    load_id.wait()
    w_id[...] = log_weight(id_count[...])

    def round_ident(c):
        rows = ids[:, column(c)].astype(BF16)
        right[half, c] = rows
        w_right[c + 1] = (rows.astype(F32) * w_id[pl.ds(c, 1), :]).astype(BF16)

    unrolled(idents, round_ident)
    right_copy(half).start()

    place = lax.broadcasted_iota(jnp.int32, (1, blocks), 1)
    code = ((place * 256 + slot_row[...] + 1) * 64 + id_row[...] + 1).astype(F32)

    def sort_by(which, key):
        order, last = sorted_codes(key[...].astype(F32), code, plan.shape[2])
        plan[which, 0:1, :] = order
        plan[which, 1:2, :] = last
        copy = pltpu.make_async_copy(plan.at[which], plan_smem.at[which], load_sem.at[3 + which])
        copy.start()
        return copy

    slot_plan = sort_by(0, slot_row)
    w_right[0] = jnp.zeros(w_right.shape[1:], BF16)
    w_left[0] = jnp.zeros(w_left.shape[1:], BF16)
    gram[0] = jnp.zeros(gram.shape[1:], F32)

    def full_right(c):
        return jnp.concatenate([right[0, c], right[1, c]], axis=0)

    def full_left(s):
        return jnp.concatenate([left[0, s], left[1, s]], axis=0)

    def right_gram(c):
        gram[c + 1] = dot_nt(w_right[c + 1], full_right(c))


    def running_sums(which, pairs, terms, sums):
        def one(place):
            code = plan_smem[which, 0, place]
            return within(code >> 15, blocks), within((code >> 7) & 255, peers + 1), within(
                (code >> 1) & 63, idents + 1
            )

        def step(i, carry):
            for u in range(width):
                p = i * width + u
                keep = (plan_smem[which, 0, 2 * p] & 1).astype(F32)
                new = terms(one(2 * p), one(2 * p + 1))
                carry = tuple(acc * keep + term for acc, term in zip(carry, new))
                for ref, acc in zip(sums, carry):
                    ref[p] = acc
            return carry

        width = pairs // ROUNDS
        zero = tuple(jnp.zeros(ref.shape[1:], F32) for ref in sums)
        lax.fori_loop(0, ROUNDS, step, zero)

    def slot_product(first, second):
        (b0, _, c0), (b1, _, c1) = first, second
        factors = jnp.concatenate([w_right[c0], w_right[c1]], axis=1)
        values = jnp.concatenate([obs[b0], obs[b1]], axis=1)
        return (dot_nt(factors, values),)

    def slot_gram(first, second):
        return (gram[first[2]] + gram[second[2]],)

    def id_terms(first, second):
        (b0, s0, _), (b1, s1, _) = first, second
        factors = jnp.concatenate([w_left[s0], w_left[s1]], axis=1)
        values = jnp.concatenate([obs[b0], obs[b1]], axis=0)
        return dot_nn(factors, values), gram[s0] + gram[s1]

    slot_plan.wait()
    load_obs.wait()
    running_sums(0, pairs_for(blocks, peers), slot_product, (total,))
    right_copy(other).wait_recv()
    unrolled(idents, right_gram)

    @pl.loop(1, peers)
    def _(step):
        source = lax.rem(me - step + peers, peers)
        left_copy(source, source).wait_recv()
        weight_copy(source, source).wait_recv()
        forward_copy(source, half).start()

    running_sums(0, pairs_for(blocks, peers), slot_gram, (total_gram,))

    def finish_slot(s):
        last = within(plan_smem[0, 1, s] >> 1, total.shape[0])
        score = dot_nn(total_gram[last].astype(BF16), full_left(s))
        back[s] = ((score - total[last]) * weight_got[s]).astype(BF16)

    def left_factors(s):
        rows = (left[half, s].astype(F32) * weight_got[s]).astype(BF16)
        w_left[s + 1] = rows
        gram[s + 1] = dot_nt(rows, full_left(s))

    @pl.loop(0, peers // GROUP)
    def _(i):
        sources = [lax.rem(me - (i * GROUP + u) + peers, peers) for u in range(GROUP)]
        for source in sources:
            forward_copy(source, other).wait_recv()
        for source in sources:
            finish_slot(source)
        for u, source in enumerate(sources):
            if u > 0:
                back_copy(source, me).start()
            else:

                @pl.when(i > 0)
                def _():
                    back_copy(source, me).start()

    id_plan = sort_by(1, id_row)
    ret[me] = back[me]
    unrolled(peers, left_factors)
    id_plan.wait()
    running_sums(1, pairs_for(blocks, idents), id_terms, (total, total_gram))

    def finish_ident(c):
        at = within(plan_smem[1, 1, c] >> 1, total.shape[0])
        used = (plan_smem[1, 1, c] & 1).astype(F32)
        score = dot_nn(total_gram[at].astype(BF16), full_right(c))
        grad = (score - total[at]) * (w_id[pl.ds(c, 1), :] * used)
        old = ids[:, column(c)]
        new_ids[:, column(c)] = old - RATE * (grad + DECAY * old)

    unrolled(idents, finish_ident)
    store_id = pltpu.make_async_copy(new_ids, new_id_out, load_sem.at[1])
    store_id.start()

    @pl.loop(1, peers)
    def _(step):
        source = lax.rem(me - step + peers, peers)
        back_copy(source, source).wait_recv()

    store_ret = pltpu.make_async_copy(ret, ret_out, load_sem.at[0])
    store_ret.start()

    right_copy(half).wait_send()
    forward_copy(me, half).wait_send()

    @pl.loop(1, peers)
    def _(step):
        peer = lax.rem(me + step, peers)
        left_copy(peer, me).wait_send()
        weight_copy(peer, me).wait_send()
        forward_copy(peer, half).wait_send()
        back_copy(peer, me).wait_send()

    store_id.wait()
    store_ret.wait()


def exchange(send_list, slot_of_block, id_of_block, rec_count, id_count, rec_t, id_t, obs):
    peers = lax.axis_size("gx")
    half_cols = rec_t.shape[0]
    blocks, blk, _ = obs.shape
    idents = id_count.shape[0]
    pairs = pairs_for(blocks, max(peers, idents))
    lanes = -(-2 * pairs // 128) * 128
    smem = pl.BlockSpec(memory_space=pltpu.SMEM)
    vmem = pl.BlockSpec(memory_space=pltpu.VMEM)
    hbm = pl.BlockSpec(memory_space=pltpu.HBM)
    anywhere = pl.BlockSpec(memory_space=pl.ANY)
    dma = pltpu.SemaphoreType.DMA
    return pl.pallas_call(
        exchange_kernel,
        out_shape=(
            jax.ShapeDtypeStruct((peers, half_cols, blk), BF16),
            jax.ShapeDtypeStruct(id_t.shape, F32),
        ),
        in_specs=[smem] + [vmem] * 4 + [hbm] * 3,
        out_specs=(anywhere, anywhere),
        scratch_shapes=[
            pltpu.VMEM(rec_t.shape, F32),
            pltpu.VMEM((rec_count.shape[0], half_cols, blk), BF16),
            pltpu.VMEM(id_t.shape, F32),
            pltpu.VMEM(id_t.shape, F32),
            pltpu.VMEM(obs.shape, BF16),
            pltpu.VMEM((rec_count.shape[0], 1, blk), F32),
            pltpu.VMEM(id_count.shape, F32),
            pltpu.VMEM((2, peers, half_cols, blk), BF16),
            pltpu.VMEM((2, idents, half_cols, blk), BF16),
            pltpu.VMEM((idents + 1, half_cols, blk), BF16),
            pltpu.VMEM((peers + 1, half_cols, blk), BF16),
            pltpu.VMEM((max(idents, peers) + 1, half_cols, 2 * half_cols), F32),
            pltpu.VMEM((peers, half_cols, blk), BF16),
            pltpu.VMEM((peers, 1, blk), F32),
            pltpu.VMEM((peers, 1, blk), F32),
            pltpu.VMEM((peers, half_cols, blk), BF16),
            pltpu.VMEM((peers, half_cols, blk), BF16),
            pltpu.VMEM((pairs, half_cols, blk), F32),
            pltpu.VMEM((pairs, half_cols, 2 * half_cols), F32),
            pltpu.VMEM((2, 8, lanes), jnp.int32),
            pltpu.SMEM((2, 8, lanes), jnp.int32),
            dma((5,)),
        ]
        + [dma((peers,))] * 8
        + [dma, dma],
        compiler_params=pltpu.CompilerParams(
            collective_id=0, has_side_effects=True, vmem_limit_bytes=VMEM_BYTES
        ),
        name="exchange",
    )(
        send_list, slot_of_block[None], id_of_block[None],
        rec_count, id_count, rec_t, id_t, obs,
    )


def update_kernel(
    send_list, rec_in, ret_in, new_id, new_rec, id_out, rec, ret, ids, sem, parts
):
    blk = ret.shape[2]
    width = rec.shape[1] // PARTS

    def part(k):
        return pl.ds(k * width, width)

    def load(k):
        return pltpu.make_async_copy(rec_in.at[:, part(k)], rec.at[:, part(k)], parts.at[k])

    def store(k):
        return pltpu.make_async_copy(rec.at[:, part(k)], new_rec.at[:, part(k)], parts.at[k])

    load_ret = pltpu.make_async_copy(ret_in, ret, sem.at[0])
    load_id = pltpu.make_async_copy(new_id, ids, sem.at[1])
    store_id = pltpu.make_async_copy(ids, id_out, sem.at[1])
    for k in range(PARTS):
        load(k).start()
    load_ret.start()
    load_id.start()
    shrink = 1.0 - RATE * DECAY
    for k in range(PARTS):
        load(k).wait()
        rec[:, part(k)] = rec[:, part(k)] * shrink
    load_ret.wait()

    @pl.loop(0, ret.shape[0])
    def _(s):
        cols = pl.ds(pl.multiple_of(send_list[s] * blk, blk), blk)
        rec[:, cols] = rec[:, cols] - RATE * ret[s].astype(F32)

    for k in range(PARTS):
        store(k).start()
    load_id.wait()
    store_id.start()
    for k in range(PARTS):
        store(k).wait()
    store_id.wait()


def update(send_list, rec_t, ret, new_id):
    hbm = pl.BlockSpec(memory_space=pltpu.HBM)
    anywhere = pl.BlockSpec(memory_space=pl.ANY)
    dma = pltpu.SemaphoreType.DMA
    return pl.pallas_call(
        update_kernel,
        out_shape=(
            jax.ShapeDtypeStruct(rec_t.shape, F32),
            jax.ShapeDtypeStruct(new_id.shape, F32),
        ),
        in_specs=[pl.BlockSpec(memory_space=pltpu.SMEM)] + [anywhere] * 3,
        out_specs=(hbm, hbm),
        scratch_shapes=[
            pltpu.VMEM(rec_t.shape, F32),
            pltpu.VMEM(ret.shape, BF16),
            pltpu.VMEM(new_id.shape, F32),
            dma((2,)),
            dma((PARTS,)),
        ],
        compiler_params=pltpu.CompilerParams(vmem_limit_bytes=VMEM_BYTES),
        name="update",
    )(send_list, rec_t, ret, new_id)


def body(records, idents, rec_count, id_count, observed, send_list, slot_of_block, id_of_block):
    blk = observed.shape[1]
    wanted = send_list.reshape(-1)
    rec_t = records.T
    ret, new_id = exchange(
        wanted,
        slot_of_block,
        id_of_block,
        rec_count.reshape(-1, blk),
        id_count.reshape(-1, blk),
        rec_t,
        idents.T,
        observed,
    )
    new_rec, new_id = update(wanted, rec_t, ret, new_id)
    return new_rec.T, new_id.T


def solution(mesh):
    in_specs = (
        P("gx", "gy"),
        P("gx", "gy"),
        P("gx"),
        P("gx"),
        P("gx", None, None),
        P("gx", None),
        P("gx"),
        P("gx"),
    )
    out_specs = (P("gx", "gy"), P("gx", "gy"))
    return jax.shard_map(body, mesh=mesh, in_specs=in_specs, out_specs=out_specs, check_vma=False)
```

```python
import jax
import jax.numpy as jnp
from jax import lax
from jax.experimental import pallas as pl
from jax.experimental.pallas import tpu as pltpu
from jax.sharding import PartitionSpec as P

MESH = pl.DeviceIdType.MESH
RATE = 0.05
DECAY = 0.1
UNROLL = 8
GROUP = 8
ROUNDS = 4
WAVE = 4
PARTS = 4
VMEM_BYTES = 58 << 20
F32 = jnp.float32
BF16 = jnp.bfloat16


def dot_nn(a, b):
    return lax.dot_general(a, b, (((1,), (0,)), ((), ())), preferred_element_type=F32)


def dot_nt(a, b):
    return lax.dot_general(a, b, (((1,), (1,)), ((), ())), preferred_element_type=F32)


def log_weight(count):
    return jnp.log(1.0 + count.astype(F32)) / jnp.log(F32(1001.0))


def pairs_for(blocks, keys):
    return -(-(blocks + keys) // (2 * UNROLL)) * UNROLL


def column_of(row):
    size = row.shape[1]
    diagonal = lax.broadcasted_iota(jnp.int32, (size, size), 0) == lax.broadcasted_iota(
        jnp.int32, (size, size), 1
    )
    return jnp.sum(jnp.where(diagonal, row, 0.0), axis=1, keepdims=True)


def sorted_codes(key, payload, lanes):
    size = key.shape[1]
    across = lax.broadcasted_iota(jnp.int32, (size, size), 1)
    down = lax.broadcasted_iota(jnp.int32, (size, size), 0)
    key_col = column_of(key)
    equal = jnp.where(key == key_col, 1.0, 0.0)

    def places(count, earlier):
        odd = count - 2.0 * jnp.floor(0.5 * count)
        return 1.0 + jnp.where(earlier == 0.0, odd, 0.0)

    earlier = jnp.sum(jnp.where(across < down, equal, 0.0), axis=1, keepdims=True)
    places_col = places(jnp.sum(equal, axis=1, keepdims=True), earlier)
    earlier_row = jnp.sum(jnp.where(down < across, equal, 0.0), axis=0, keepdims=True)
    places_row = places(jnp.sum(equal, axis=0, keepdims=True), earlier_row)
    smaller = jnp.where(key < key_col, places_row, 0.0)
    rank = earlier + jnp.sum(smaller, axis=1, keepdims=True)
    marked = 2.0 * column_of(payload) + jnp.minimum(earlier, 1.0)
    value = lax.broadcasted_iota(jnp.int32, (1, lanes), 1).astype(F32)
    order = jnp.sum(jnp.where(rank == value, marked, 0.0), axis=0, keepdims=True)
    up_to = jnp.sum(jnp.where(key_col <= value, places_col, 0.0), axis=0, keepdims=True)
    used = jnp.sum(jnp.where(key_col == value, 1.0, 0.0), axis=0, keepdims=True)
    last = 2.0 * jnp.maximum(0.5 * up_to - 1.0, 0.0) + jnp.minimum(used, 1.0)
    return order.astype(jnp.int32), last.astype(jnp.int32)


def exchange_kernel(
    send_list, slot_row, id_row, rec_count, id_count,
    rec_hbm, id_hbm, obs_hbm,
    ret_out, new_id_out,
    rec, rec_bf, ids, new_ids, obs, w_rec, w_id, left, right, w_right, w_left, gram,
    left_send, weight_send, weight_got, back, ret, total, total_gram,
    plan, plan_smem, load_sem, ls, lr, ws, wr, fs, fr, bs, br, rs, rr,
):
    peers = lax.axis_size("gx")
    me = lax.axis_index("gx")
    half = lax.axis_index("gy")
    other = 1 - half
    idents = id_count.shape[0]
    blocks = obs.shape[0]
    blk = obs.shape[1]

    load_rec = pltpu.make_async_copy(rec_hbm, rec, load_sem.at[0])
    load_id = pltpu.make_async_copy(id_hbm, ids, load_sem.at[1])
    load_obs = pltpu.make_async_copy(obs_hbm, obs, load_sem.at[2])
    load_rec.start()
    load_id.start()
    barrier = pltpu.get_barrier_semaphore()

    @pl.loop(1, peers)
    def _(step):
        pl.semaphore_signal(
            barrier, inc=1, device_id={"gx": lax.rem(me + step, peers)}, device_id_type=MESH
        )

    pl.semaphore_signal(barrier, inc=1, device_id={"gy": other}, device_id_type=MESH)

    weights = log_weight(rec_count[...]).astype(BF16).astype(F32)
    for r in range(weights.shape[0]):
        w_rec[r] = weights[r : r + 1, :]

    def within(index, count):
        return jnp.clip(index, 0, count - 1)

    def column(block):
        return pl.ds(pl.multiple_of(block * blk, blk), blk)

    def unrolled(count, function):
        @pl.loop(0, count // GROUP)
        def _(i):
            for u in range(GROUP):
                function(i * GROUP + u)

    load_rec.wait()
    load_obs.start()

    def round_record(r):
        rec_bf[r] = rec[:, column(r)].astype(BF16)

    unrolled(rec_bf.shape[0], round_record)

    @pl.loop(0, peers)
    def _(peer):
        wanted = send_list[peer]
        left_send[peer] = rec_bf[wanted]
        weight_send[peer] = w_rec[wanted]

    left[half, me] = left_send[me]
    weight_got[me] = weight_send[me]
    pl.semaphore_wait(barrier, peers)

    def left_copy(peer, slot):
        return pltpu.make_async_remote_copy(
            src_ref=left_send.at[peer], dst_ref=left.at[half, slot],
            send_sem=ls.at[peer], recv_sem=lr.at[slot],
            device_id={"gx": peer}, device_id_type=MESH,
        )

    def weight_copy(peer, slot):
        return pltpu.make_async_remote_copy(
            src_ref=weight_send.at[peer], dst_ref=weight_got.at[slot],
            send_sem=ws.at[peer], recv_sem=wr.at[slot],
            device_id={"gx": peer}, device_id_type=MESH,
        )

    def forward_copy(slot, side):
        return pltpu.make_async_remote_copy(
            src_ref=left.at[side, slot], dst_ref=left.at[side, slot],
            send_sem=fs.at[slot], recv_sem=fr.at[slot],
            device_id={"gy": other}, device_id_type=MESH,
        )

    def back_copy(peer, slot):
        return pltpu.make_async_remote_copy(
            src_ref=back.at[peer], dst_ref=ret.at[slot],
            send_sem=bs.at[peer], recv_sem=br.at[slot],
            device_id={"gx": peer}, device_id_type=MESH,
        )

    def right_copy(side):
        return pltpu.make_async_remote_copy(
            src_ref=right.at[side], dst_ref=right.at[side],
            send_sem=rs, recv_sem=rr,
            device_id={"gy": other}, device_id_type=MESH,
        )

    def distance(step):
        return 1 + lax.rem(step - 1 + peers // 4 - 1, peers - 1)

    @pl.loop(1, peers)
    def _(step):
        peer = lax.rem(me + distance(step), peers)
        left_copy(peer, me).start()
        weight_copy(peer, me).start()

    forward_copy(me, half).start()
    load_id.wait()
    w_id[...] = log_weight(id_count[...])

    def round_ident(c):
        rows = ids[:, column(c)].astype(BF16)
        right[half, c] = rows
        w_right[c + 1] = (rows.astype(F32) * w_id[pl.ds(c, 1), :]).astype(BF16)

    unrolled(idents, round_ident)
    right_copy(half).start()

    place = lax.broadcasted_iota(jnp.int32, (1, blocks), 1)
    code = ((place * 256 + slot_row[...] + 1) * 64 + id_row[...] + 1).astype(F32)

    def sort_by(which, key):
        order, last = sorted_codes(key[...].astype(F32), code, plan.shape[2])
        plan[which, 0:1, :] = order
        plan[which, 1:2, :] = last
        copy = pltpu.make_async_copy(plan.at[which], plan_smem.at[which], load_sem.at[3 + which])
        copy.start()
        return copy

    slot_plan = sort_by(0, slot_row)
    w_right[0] = jnp.zeros(w_right.shape[1:], BF16)
    w_left[0] = jnp.zeros(w_left.shape[1:], BF16)
    gram[0] = jnp.zeros(gram.shape[1:], F32)

    def full_right(c):
        return jnp.concatenate([right[0, c], right[1, c]], axis=0)

    def full_left(s):
        return jnp.concatenate([left[0, s], left[1, s]], axis=0)

    def right_gram(c):
        gram[c + 1] = dot_nt(w_right[c + 1], full_right(c))


    def running_sums(which, pairs, terms, sums):
        def one(place):
            code = plan_smem[which, 0, place]
            return within(code >> 15, blocks), within((code >> 7) & 255, peers + 1), within(
                (code >> 1) & 63, idents + 1
            )

        def step(i, carry):
            for u in range(width):
                p = i * width + u
                keep = (plan_smem[which, 0, 2 * p] & 1).astype(F32)
                new = terms(one(2 * p), one(2 * p + 1))
                carry = tuple(acc * keep + term for acc, term in zip(carry, new))
                for ref, acc in zip(sums, carry):
                    ref[p] = acc
            return carry

        width = pairs // ROUNDS
        zero = tuple(jnp.zeros(ref.shape[1:], F32) for ref in sums)
        lax.fori_loop(0, ROUNDS, step, zero)

    def slot_product(first, second):
        (b0, _, c0), (b1, _, c1) = first, second
        factors = jnp.concatenate([w_right[c0], w_right[c1]], axis=1)
        values = jnp.concatenate([obs[b0], obs[b1]], axis=1)
        return (dot_nt(factors, values),)

    def slot_gram(first, second):
        return (gram[first[2]] + gram[second[2]],)

    def id_terms(first, second):
        (b0, s0, _), (b1, s1, _) = first, second
        factors = jnp.concatenate([w_left[s0], w_left[s1]], axis=1)
        values = jnp.concatenate([obs[b0], obs[b1]], axis=0)
        return dot_nn(factors, values), gram[s0] + gram[s1]

    slot_plan.wait()
    load_obs.wait()
    running_sums(0, pairs_for(blocks, peers), slot_product, (total,))
    right_copy(other).wait_recv()
    unrolled(idents, right_gram)

    running_sums(0, pairs_for(blocks, peers), slot_gram, (total_gram,))

    def finish_slot(s):
        last = within(plan_smem[0, 1, s] >> 1, total.shape[0])
        score = dot_nn(total_gram[last].astype(BF16), full_left(s))
        back[s] = ((score - total[last]) * weight_got[s]).astype(BF16)

    def left_factors(s):
        rows = (left[half, s].astype(F32) * weight_got[s]).astype(BF16)
        w_left[s + 1] = rows
        gram[s + 1] = dot_nt(rows, full_left(s))

    def source_of(step):
        return lax.rem(me - distance(step) + peers, peers)

    @pl.loop(0, peers // WAVE + 1)
    def _(i):
        def relay(step):
            source = source_of(step)
            left_copy(source, source).wait_recv()
            weight_copy(source, source).wait_recv()
            forward_copy(source, half).start()

        @pl.when(i < peers // WAVE)
        def _():
            for u in range(1, WAVE):
                relay(i * WAVE + u)

            @pl.when(i > 0)
            def _():
                relay(i * WAVE)

        @pl.when(i > 0)
        def _():
            first = (i - 1) * WAVE
            for u in range(1, WAVE):
                forward_copy(source_of(first + u), other).wait_recv()

            @pl.when(first > 0)
            def _():
                forward_copy(source_of(first), other).wait_recv()

            @pl.when(first == 0)
            def _():
                forward_copy(me, other).wait_recv()
                finish_slot(me)

            @pl.when(first > 0)
            def _():
                finish_slot(source_of(first))
                back_copy(source_of(first), me).start()

            for u in range(1, WAVE):
                finish_slot(source_of(first + u))
            for u in range(1, WAVE):
                back_copy(source_of(first + u), me).start()

    id_plan = sort_by(1, id_row)
    ret[me] = back[me]
    unrolled(peers, left_factors)
    id_plan.wait()
    running_sums(1, pairs_for(blocks, idents), id_terms, (total, total_gram))

    def finish_ident(c):
        at = within(plan_smem[1, 1, c] >> 1, total.shape[0])
        used = (plan_smem[1, 1, c] & 1).astype(F32)
        score = dot_nn(total_gram[at].astype(BF16), full_right(c))
        grad = (score - total[at]) * (w_id[pl.ds(c, 1), :] * used)
        old = ids[:, column(c)]
        new_ids[:, column(c)] = old - RATE * (grad + DECAY * old)

    unrolled(idents, finish_ident)
    store_id = pltpu.make_async_copy(new_ids, new_id_out, load_sem.at[1])
    store_id.start()

    @pl.loop(1, peers)
    def _(step):
        source = lax.rem(me - step + peers, peers)
        back_copy(source, source).wait_recv()

    store_ret = pltpu.make_async_copy(ret, ret_out, load_sem.at[0])
    store_ret.start()

    right_copy(half).wait_send()
    forward_copy(me, half).wait_send()

    @pl.loop(1, peers)
    def _(step):
        peer = lax.rem(me + step, peers)
        left_copy(peer, me).wait_send()
        weight_copy(peer, me).wait_send()
        forward_copy(peer, half).wait_send()
        back_copy(peer, me).wait_send()

    store_id.wait()
    store_ret.wait()


def exchange(send_list, slot_of_block, id_of_block, rec_count, id_count, rec_t, id_t, obs):
    peers = lax.axis_size("gx")
    half_cols = rec_t.shape[0]
    blocks, blk, _ = obs.shape
    idents = id_count.shape[0]
    pairs = pairs_for(blocks, max(peers, idents))
    lanes = -(-2 * pairs // 128) * 128
    smem = pl.BlockSpec(memory_space=pltpu.SMEM)
    vmem = pl.BlockSpec(memory_space=pltpu.VMEM)
    hbm = pl.BlockSpec(memory_space=pltpu.HBM)
    anywhere = pl.BlockSpec(memory_space=pl.ANY)
    dma = pltpu.SemaphoreType.DMA
    return pl.pallas_call(
        exchange_kernel,
        out_shape=(
            jax.ShapeDtypeStruct((peers, half_cols, blk), BF16),
            jax.ShapeDtypeStruct(id_t.shape, F32),
        ),
        in_specs=[smem] + [vmem] * 4 + [hbm] * 3,
        out_specs=(anywhere, anywhere),
        scratch_shapes=[
            pltpu.VMEM(rec_t.shape, F32),
            pltpu.VMEM((rec_count.shape[0], half_cols, blk), BF16),
            pltpu.VMEM(id_t.shape, F32),
            pltpu.VMEM(id_t.shape, F32),
            pltpu.VMEM(obs.shape, BF16),
            pltpu.VMEM((rec_count.shape[0], 1, blk), F32),
            pltpu.VMEM(id_count.shape, F32),
            pltpu.VMEM((2, peers, half_cols, blk), BF16),
            pltpu.VMEM((2, idents, half_cols, blk), BF16),
            pltpu.VMEM((idents + 1, half_cols, blk), BF16),
            pltpu.VMEM((peers + 1, half_cols, blk), BF16),
            pltpu.VMEM((max(idents, peers) + 1, half_cols, 2 * half_cols), F32),
            pltpu.VMEM((peers, half_cols, blk), BF16),
            pltpu.VMEM((peers, 1, blk), F32),
            pltpu.VMEM((peers, 1, blk), F32),
            pltpu.VMEM((peers, half_cols, blk), BF16),
            pltpu.VMEM((peers, half_cols, blk), BF16),
            pltpu.VMEM((pairs, half_cols, blk), F32),
            pltpu.VMEM((pairs, half_cols, 2 * half_cols), F32),
            pltpu.VMEM((2, 8, lanes), jnp.int32),
            pltpu.SMEM((2, 8, lanes), jnp.int32),
            dma((5,)),
        ]
        + [dma((peers,))] * 8
        + [dma, dma],
        compiler_params=pltpu.CompilerParams(
            collective_id=0, has_side_effects=True, vmem_limit_bytes=VMEM_BYTES
        ),
        name="exchange",
    )(
        send_list, slot_of_block[None], id_of_block[None],
        rec_count, id_count, rec_t, id_t, obs,
    )


def update_kernel(
    send_list, rec_in, ret_in, new_id, new_rec, id_out, rec, ret, ids, sem, parts
):
    blk = ret.shape[2]
    width = rec.shape[1] // PARTS

    def part(k):
        return pl.ds(k * width, width)

    def load(k):
        return pltpu.make_async_copy(rec_in.at[:, part(k)], rec.at[:, part(k)], parts.at[k])

    def store(k):
        return pltpu.make_async_copy(rec.at[:, part(k)], new_rec.at[:, part(k)], parts.at[k])

    load_ret = pltpu.make_async_copy(ret_in, ret, sem.at[0])
    load_id = pltpu.make_async_copy(new_id, ids, sem.at[1])
    store_id = pltpu.make_async_copy(ids, id_out, sem.at[1])
    load_ret.start()
    load(0).start()
    load_id.start()
    for k in range(1, PARTS):
        load(k).start()
    shrink = 1.0 - RATE * DECAY
    load_ret.wait()
    for k in range(PARTS):
        load(k).wait()
        rec[:, part(k)] = rec[:, part(k)] * shrink

        @pl.loop(0, ret.shape[0])
        def _(s):
            block = send_list[s]

            @pl.when(block // (width // blk) == k)
            def _():
                cols = pl.ds(pl.multiple_of(block * blk, blk), blk)
                rec[:, cols] = rec[:, cols] - RATE * ret[s].astype(F32)

        store(k).start()
        if k == 0:
            load_id.wait()
            store_id.start()
    for k in range(PARTS):
        store(k).wait()
    store_id.wait()


def update(send_list, rec_t, ret, new_id):
    hbm = pl.BlockSpec(memory_space=pltpu.HBM)
    anywhere = pl.BlockSpec(memory_space=pl.ANY)
    dma = pltpu.SemaphoreType.DMA
    return pl.pallas_call(
        update_kernel,
        out_shape=(
            jax.ShapeDtypeStruct(rec_t.shape, F32),
            jax.ShapeDtypeStruct(new_id.shape, F32),
        ),
        in_specs=[pl.BlockSpec(memory_space=pltpu.SMEM)] + [anywhere] * 3,
        out_specs=(hbm, hbm),
        scratch_shapes=[
            pltpu.VMEM(rec_t.shape, F32),
            pltpu.VMEM(ret.shape, BF16),
            pltpu.VMEM(new_id.shape, F32),
            dma((2,)),
            dma((PARTS,)),
        ],
        compiler_params=pltpu.CompilerParams(vmem_limit_bytes=VMEM_BYTES),
        name="update",
    )(send_list, rec_t, ret, new_id)


def body(records, idents, rec_count, id_count, observed, send_list, slot_of_block, id_of_block):
    blk = observed.shape[1]
    wanted = send_list.reshape(-1)
    rec_t = records.T
    ret, new_id = exchange(
        wanted,
        slot_of_block,
        id_of_block,
        rec_count.reshape(-1, blk),
        id_count.reshape(-1, blk),
        rec_t,
        idents.T,
        observed,
    )
    new_rec, new_id = update(wanted, rec_t, ret, new_id)
    return new_rec.T, new_id.T


def solution(mesh):
    in_specs = (
        P("gx", "gy"),
        P("gx", "gy"),
        P("gx"),
        P("gx"),
        P("gx", None, None),
        P("gx", None),
        P("gx"),
        P("gx"),
    )
    out_specs = (P("gx", "gy"), P("gx", "gy"))
    return jax.shard_map(body, mesh=mesh, in_specs=in_specs, out_specs=out_specs, check_vma=False)
```

```python
import jax
import jax.numpy as jnp
from jax import lax
from jax.experimental import pallas as pl
from jax.experimental.pallas import tpu as pltpu
from jax.sharding import PartitionSpec as P

MESH = pl.DeviceIdType.MESH
RATE = 0.05
DECAY = 0.1
UNROLL = 8
GROUP = 8
ROUNDS = 4
WAVE = 4
PARTS = 4
VMEM_BYTES = 58 << 20
F32 = jnp.float32
BF16 = jnp.bfloat16


def dot_nn(a, b):
    return lax.dot_general(a, b, (((1,), (0,)), ((), ())), preferred_element_type=F32)


def dot_nt(a, b):
    return lax.dot_general(a, b, (((1,), (1,)), ((), ())), preferred_element_type=F32)


def log_weight(count):
    return jnp.log(1.0 + count.astype(F32)) / jnp.log(F32(1001.0))


def pairs_for(blocks, keys):
    return -(-(blocks + keys) // (2 * UNROLL)) * UNROLL


def column_of(row):
    size = row.shape[1]
    diagonal = lax.broadcasted_iota(jnp.int32, (size, size), 0) == lax.broadcasted_iota(
        jnp.int32, (size, size), 1
    )
    return jnp.sum(jnp.where(diagonal, row, 0.0), axis=1, keepdims=True)


def sorted_codes(key, payload, lanes):
    size = key.shape[1]
    across = lax.broadcasted_iota(jnp.int32, (size, size), 1)
    down = lax.broadcasted_iota(jnp.int32, (size, size), 0)
    key_col = column_of(key)
    equal = jnp.where(key == key_col, 1.0, 0.0)

    def places(count, earlier):
        odd = count - 2.0 * jnp.floor(0.5 * count)
        return 1.0 + jnp.where(earlier == 0.0, odd, 0.0)

    earlier = jnp.sum(jnp.where(across < down, equal, 0.0), axis=1, keepdims=True)
    places_col = places(jnp.sum(equal, axis=1, keepdims=True), earlier)
    earlier_row = jnp.sum(jnp.where(down < across, equal, 0.0), axis=0, keepdims=True)
    places_row = places(jnp.sum(equal, axis=0, keepdims=True), earlier_row)
    smaller = jnp.where(key < key_col, places_row, 0.0)
    rank = earlier + jnp.sum(smaller, axis=1, keepdims=True)
    marked = 2.0 * column_of(payload) + jnp.minimum(earlier, 1.0)
    value = lax.broadcasted_iota(jnp.int32, (1, lanes), 1).astype(F32)
    order = jnp.sum(jnp.where(rank == value, marked, 0.0), axis=0, keepdims=True)
    up_to = jnp.sum(jnp.where(key_col <= value, places_col, 0.0), axis=0, keepdims=True)
    used = jnp.sum(jnp.where(key_col == value, 1.0, 0.0), axis=0, keepdims=True)
    last = 2.0 * jnp.maximum(0.5 * up_to - 1.0, 0.0) + jnp.minimum(used, 1.0)
    return order.astype(jnp.int32), last.astype(jnp.int32)


def exchange_kernel(
    send_list, slot_row, id_row, rec_count, id_count,
    rec_hbm, id_hbm, obs_hbm,
    ret_out, new_id_out,
    rec, rec_bf, ids, new_ids, obs, w_rec, w_id, left, right, w_right, w_left, gram,
    left_send, weight_send, weight_got, back, ret, total, total_gram,
    plan, plan_smem, load_sem, ls, lr, ws, wr, fs, fr, bs, br, rs, rr,
):
    peers = lax.axis_size("gx")
    me = lax.axis_index("gx")
    half = lax.axis_index("gy")
    other = 1 - half
    idents = id_count.shape[0]
    blocks = obs.shape[0]
    blk = obs.shape[1]

    load_rec = pltpu.make_async_copy(rec_hbm, rec, load_sem.at[0])
    load_id = pltpu.make_async_copy(id_hbm, ids, load_sem.at[1])
    load_obs = pltpu.make_async_copy(obs_hbm, obs, load_sem.at[2])
    load_rec.start()
    load_id.start()
    barrier = pltpu.get_barrier_semaphore()

    @pl.loop(1, peers)
    def _(step):
        pl.semaphore_signal(
            barrier, inc=1, device_id={"gx": lax.rem(me + step, peers)}, device_id_type=MESH
        )

    pl.semaphore_signal(barrier, inc=1, device_id={"gy": other}, device_id_type=MESH)

    weights = log_weight(rec_count[...]).astype(BF16).astype(F32)
    for r in range(weights.shape[0]):
        w_rec[r] = weights[r : r + 1, :]

    def within(index, count):
        return jnp.clip(index, 0, count - 1)

    def column(block):
        return pl.ds(pl.multiple_of(block * blk, blk), blk)

    def unrolled(count, function):
        @pl.loop(0, count // GROUP)
        def _(i):
            for u in range(GROUP):
                function(i * GROUP + u)

    load_rec.wait()
    load_obs.start()

    def round_record(r):
        rec_bf[r] = rec[:, column(r)].astype(BF16)

    unrolled(rec_bf.shape[0], round_record)

    @pl.loop(0, peers)
    def _(peer):
        wanted = send_list[peer]
        left_send[peer] = rec_bf[wanted]
        weight_send[peer] = w_rec[wanted]

    left[half, me] = left_send[me]
    weight_got[me] = weight_send[me]
    pl.semaphore_wait(barrier, peers)

    def left_copy(peer, slot):
        return pltpu.make_async_remote_copy(
            src_ref=left_send.at[peer], dst_ref=left.at[half, slot],
            send_sem=ls.at[peer], recv_sem=lr.at[slot],
            device_id={"gx": peer}, device_id_type=MESH,
        )

    def weight_copy(peer, slot):
        return pltpu.make_async_remote_copy(
            src_ref=weight_send.at[peer], dst_ref=weight_got.at[slot],
            send_sem=ws.at[peer], recv_sem=wr.at[slot],
            device_id={"gx": peer}, device_id_type=MESH,
        )

    def forward_copy(slot, side):
        return pltpu.make_async_remote_copy(
            src_ref=left.at[side, slot], dst_ref=left.at[side, slot],
            send_sem=fs.at[slot], recv_sem=fr.at[slot],
            device_id={"gy": other}, device_id_type=MESH,
        )

    def back_copy(peer, slot):
        return pltpu.make_async_remote_copy(
            src_ref=back.at[peer], dst_ref=ret.at[slot],
            send_sem=bs.at[peer], recv_sem=br.at[slot],
            device_id={"gx": peer}, device_id_type=MESH,
        )

    def right_copy(side):
        return pltpu.make_async_remote_copy(
            src_ref=right.at[side], dst_ref=right.at[side],
            send_sem=rs, recv_sem=rr,
            device_id={"gy": other}, device_id_type=MESH,
        )

    def distance(step):
        return 1 + lax.rem(step - 1 + peers // 4 - 1, peers - 1)

    @pl.loop(1, peers)
    def _(step):
        peer = lax.rem(me + distance(step), peers)
        left_copy(peer, me).start()
        weight_copy(peer, me).start()

    forward_copy(me, half).start()
    load_id.wait()
    w_id[...] = log_weight(id_count[...])

    def round_ident(c):
        rows = ids[:, column(c)].astype(BF16)
        right[half, c] = rows
        w_right[c + 1] = (rows.astype(F32) * w_id[pl.ds(c, 1), :]).astype(BF16)

    unrolled(idents, round_ident)
    right_copy(half).start()

    place = lax.broadcasted_iota(jnp.int32, (1, blocks), 1)
    code = ((place * 256 + slot_row[...] + 1) * 64 + id_row[...] + 1).astype(F32)

    def sort_by(which, key):
        order, last = sorted_codes(key[...].astype(F32), code, plan.shape[2])
        plan[which, 0:1, :] = order
        plan[which, 1:2, :] = last
        copy = pltpu.make_async_copy(plan.at[which], plan_smem.at[which], load_sem.at[3 + which])
        copy.start()
        return copy

    slot_plan = sort_by(0, slot_row)
    w_right[0] = jnp.zeros(w_right.shape[1:], BF16)
    w_left[0] = jnp.zeros(w_left.shape[1:], BF16)
    gram[0] = jnp.zeros(gram.shape[1:], F32)

    def full_right(c):
        return jnp.concatenate([right[0, c], right[1, c]], axis=0)

    def full_left(s):
        return jnp.concatenate([left[0, s], left[1, s]], axis=0)

    def right_gram(c):
        gram[c + 1] = dot_nt(w_right[c + 1], full_right(c))


    def running_sums(which, pairs, terms, sums):
        def one(place):
            code = plan_smem[which, 0, place]
            return within(code >> 15, blocks), within((code >> 7) & 255, peers + 1), within(
                (code >> 1) & 63, idents + 1
            )

        def step(i, carry):
            for u in range(width):
                p = i * width + u
                keep = (plan_smem[which, 0, 2 * p] & 1).astype(F32)
                new = terms(one(2 * p), one(2 * p + 1))
                carry = tuple(acc * keep + term for acc, term in zip(carry, new))
                for ref, acc in zip(sums, carry):
                    ref[p] = acc
            return carry

        width = pairs // ROUNDS
        zero = tuple(jnp.zeros(ref.shape[1:], F32) for ref in sums)
        lax.fori_loop(0, ROUNDS, step, zero)

    def slot_product(first, second):
        (b0, _, c0), (b1, _, c1) = first, second
        factors = jnp.concatenate([w_right[c0], w_right[c1]], axis=1)
        values = jnp.concatenate([obs[b0], obs[b1]], axis=1)
        return (dot_nt(factors, values),)

    def slot_gram(first, second):
        return (gram[first[2]] + gram[second[2]],)

    def id_terms(first, second):
        (b0, s0, _), (b1, s1, _) = first, second
        factors = jnp.concatenate([w_left[s0], w_left[s1]], axis=1)
        values = jnp.concatenate([obs[b0], obs[b1]], axis=0)
        return dot_nn(factors, values), gram[s0] + gram[s1]

    slot_plan.wait()
    load_obs.wait()
    running_sums(0, pairs_for(blocks, peers), slot_product, (total,))
    right_copy(other).wait_recv()
    unrolled(idents, right_gram)

    running_sums(0, pairs_for(blocks, peers), slot_gram, (total_gram,))

    def finish_slot(s):
        last = within(plan_smem[0, 1, s] >> 1, total.shape[0])
        score = dot_nn(total_gram[last].astype(BF16), full_left(s))
        back[s] = ((score - total[last]) * weight_got[s]).astype(BF16)

    def left_factors(s):
        rows = (left[half, s].astype(F32) * weight_got[s]).astype(BF16)
        w_left[s + 1] = rows
        gram[s + 1] = dot_nt(rows, full_left(s))

    def source_of(step):
        return lax.rem(me - distance(step) + peers, peers)

    @pl.loop(0, peers // WAVE + 1)
    def _(i):
        def relay(step):
            source = source_of(step)
            left_copy(source, source).wait_recv()
            weight_copy(source, source).wait_recv()
            forward_copy(source, half).start()

        @pl.when(i < peers // WAVE)
        def _():
            for u in range(1, WAVE):
                relay(i * WAVE + u)

            @pl.when(i > 0)
            def _():
                relay(i * WAVE)

        @pl.when(i > 0)
        def _():
            first = (i - 1) * WAVE
            for u in range(1, WAVE):
                forward_copy(source_of(first + u), other).wait_recv()

            @pl.when(first > 0)
            def _():
                forward_copy(source_of(first), other).wait_recv()

            @pl.when(first == 0)
            def _():
                forward_copy(me, other).wait_recv()
                finish_slot(me)

            @pl.when(first > 0)
            def _():
                finish_slot(source_of(first))
                back_copy(source_of(first), me).start()

            for u in range(1, WAVE):
                finish_slot(source_of(first + u))
            for u in range(1, WAVE):
                back_copy(source_of(first + u), me).start()

    id_plan = sort_by(1, id_row)
    ret[me] = back[me]
    unrolled(peers, left_factors)
    id_plan.wait()
    running_sums(1, pairs_for(blocks, idents), id_terms, (total, total_gram))

    def finish_ident(c):
        at = within(plan_smem[1, 1, c] >> 1, total.shape[0])
        used = (plan_smem[1, 1, c] & 1).astype(F32)
        score = dot_nn(total_gram[at].astype(BF16), full_right(c))
        grad = (score - total[at]) * (w_id[pl.ds(c, 1), :] * used)
        old = ids[:, column(c)]
        new_ids[:, column(c)] = old - RATE * (grad + DECAY * old)

    unrolled(idents, finish_ident)
    store_id = pltpu.make_async_copy(new_ids, new_id_out, load_sem.at[1])
    store_id.start()

    @pl.loop(1, peers)
    def _(step):
        source = lax.rem(me - step + peers, peers)
        back_copy(source, source).wait_recv()

    store_ret = pltpu.make_async_copy(ret, ret_out, load_sem.at[0])
    store_ret.start()

    right_copy(half).wait_send()
    forward_copy(me, half).wait_send()

    @pl.loop(1, peers)
    def _(step):
        peer = lax.rem(me + step, peers)
        left_copy(peer, me).wait_send()
        weight_copy(peer, me).wait_send()
        forward_copy(peer, half).wait_send()
        back_copy(peer, me).wait_send()

    store_id.wait()
    store_ret.wait()


def exchange(send_list, slot_of_block, id_of_block, rec_count, id_count, rec_t, id_t, obs):
    peers = lax.axis_size("gx")
    half_cols = rec_t.shape[0]
    blocks, blk, _ = obs.shape
    idents = id_count.shape[0]
    pairs = pairs_for(blocks, max(peers, idents))
    lanes = -(-2 * pairs // 128) * 128
    smem = pl.BlockSpec(memory_space=pltpu.SMEM)
    vmem = pl.BlockSpec(memory_space=pltpu.VMEM)
    hbm = pl.BlockSpec(memory_space=pltpu.HBM)
    anywhere = pl.BlockSpec(memory_space=pl.ANY)
    dma = pltpu.SemaphoreType.DMA
    return pl.pallas_call(
        exchange_kernel,
        out_shape=(
            jax.ShapeDtypeStruct((peers, half_cols, blk), BF16),
            jax.ShapeDtypeStruct(id_t.shape, F32),
        ),
        in_specs=[smem] + [vmem] * 4 + [hbm] * 3,
        out_specs=(anywhere, anywhere),
        scratch_shapes=[
            pltpu.VMEM(rec_t.shape, F32),
            pltpu.VMEM((rec_count.shape[0], half_cols, blk), BF16),
            pltpu.VMEM(id_t.shape, F32),
            pltpu.VMEM(id_t.shape, F32),
            pltpu.VMEM(obs.shape, BF16),
            pltpu.VMEM((rec_count.shape[0], 1, blk), F32),
            pltpu.VMEM(id_count.shape, F32),
            pltpu.VMEM((2, peers, half_cols, blk), BF16),
            pltpu.VMEM((2, idents, half_cols, blk), BF16),
            pltpu.VMEM((idents + 1, half_cols, blk), BF16),
            pltpu.VMEM((peers + 1, half_cols, blk), BF16),
            pltpu.VMEM((max(idents, peers) + 1, half_cols, 2 * half_cols), F32),
            pltpu.VMEM((peers, half_cols, blk), BF16),
            pltpu.VMEM((peers, 1, blk), F32),
            pltpu.VMEM((peers, 1, blk), F32),
            pltpu.VMEM((peers, half_cols, blk), BF16),
            pltpu.VMEM((peers, half_cols, blk), BF16),
            pltpu.VMEM((pairs, half_cols, blk), F32),
            pltpu.VMEM((pairs, half_cols, 2 * half_cols), F32),
            pltpu.VMEM((2, 8, lanes), jnp.int32),
            pltpu.SMEM((2, 8, lanes), jnp.int32),
            dma((5,)),
        ]
        + [dma((peers,))] * 8
        + [dma, dma],
        compiler_params=pltpu.CompilerParams(
            collective_id=0, has_side_effects=True, vmem_limit_bytes=VMEM_BYTES
        ),
        name="exchange",
    )(
        send_list, slot_of_block[None], id_of_block[None],
        rec_count, id_count, rec_t, id_t, obs,
    )


def update_kernel(
    send_list, rec_in, ret_in, new_id, new_rec, id_out, rec, ret, ids, sem, parts
):
    blk = ret.shape[2]
    width = rec.shape[1] // PARTS

    def part(k):
        return pl.ds(k * width, width)

    def load(k):
        return pltpu.make_async_copy(rec_in.at[:, part(k)], rec.at[:, part(k)], parts.at[k])

    def store(k):
        return pltpu.make_async_copy(rec.at[:, part(k)], new_rec.at[:, part(k)], parts.at[k])

    load_ret = pltpu.make_async_copy(ret_in, ret, sem.at[0])
    load_id = pltpu.make_async_copy(new_id, ids, sem.at[1])
    store_id = pltpu.make_async_copy(ids, id_out, sem.at[1])
    load_ret.start()
    load(0).start()
    load_id.start()
    for k in range(1, PARTS):
        load(k).start()
    shrink = 1.0 - RATE * DECAY
    for k in range(PARTS):
        load(k).wait()
        rec[:, part(k)] = rec[:, part(k)] * shrink
    load_id.wait()
    store_id.start()
    load_ret.wait()

    @pl.loop(0, ret.shape[0] // GROUP)
    def _(i):
        for u in range(GROUP):
            s = i * GROUP + u
            cols = pl.ds(pl.multiple_of(send_list[s] * blk, blk), blk)
            rec[:, cols] = rec[:, cols] - RATE * ret[s].astype(F32)

    for k in range(PARTS):
        store(k).start()
    for k in range(PARTS):
        store(k).wait()
    store_id.wait()


def update(send_list, rec_t, ret, new_id):
    hbm = pl.BlockSpec(memory_space=pltpu.HBM)
    anywhere = pl.BlockSpec(memory_space=pl.ANY)
    dma = pltpu.SemaphoreType.DMA
    return pl.pallas_call(
        update_kernel,
        out_shape=(
            jax.ShapeDtypeStruct(rec_t.shape, F32),
            jax.ShapeDtypeStruct(new_id.shape, F32),
        ),
        in_specs=[pl.BlockSpec(memory_space=pltpu.SMEM)] + [anywhere] * 3,
        out_specs=(hbm, hbm),
        scratch_shapes=[
            pltpu.VMEM(rec_t.shape, F32),
            pltpu.VMEM(ret.shape, BF16),
            pltpu.VMEM(new_id.shape, F32),
            dma((2,)),
            dma((PARTS,)),
        ],
        compiler_params=pltpu.CompilerParams(vmem_limit_bytes=VMEM_BYTES),
        name="update",
    )(send_list, rec_t, ret, new_id)


def body(records, idents, rec_count, id_count, observed, send_list, slot_of_block, id_of_block):
    blk = observed.shape[1]
    wanted = send_list.reshape(-1)
    rec_t = records.T
    ret, new_id = exchange(
        wanted,
        slot_of_block,
        id_of_block,
        rec_count.reshape(-1, blk),
        id_count.reshape(-1, blk),
        rec_t,
        idents.T,
        observed,
    )
    new_rec, new_id = update(wanted, rec_t, ret, new_id)
    return new_rec.T, new_id.T


def solution(mesh):
    in_specs = (
        P("gx", "gy"),
        P("gx", "gy"),
        P("gx"),
        P("gx"),
        P("gx", None, None),
        P("gx", None),
        P("gx"),
        P("gx"),
    )
    out_specs = (P("gx", "gy"), P("gx", "gy"))
    return jax.shard_map(body, mesh=mesh, in_specs=in_specs, out_specs=out_specs, check_vma=False)
```
